256 devices in a mesh: ctx: 16 (over y, x), sub: 16 (over z, core).
Axes of the slice: x: 4, y: 4, z: 8, core: 2. Of those that a mesh axis runs over, the one named last changes fastest.
Arguments:
- stream: bfloat16 [65536, 1536], P(('ctx', 'sub')), may hold values from -18 to 18
- query_full: bfloat16 [65536, 1536], P(('ctx', 'sub')), may hold values from -122 to 122
- key_full: bfloat16 [65536, 1536], P(('ctx', 'sub')), may hold values from -6 to 6
- value_full: bfloat16 [65536, 1536], P(('ctx', 'sub')), may hold values from -6 to 6
- pool_fine: float32 [4, 1536], replicated, may hold values from -3 to 3
- pool_coarse: float32 [4, 1536], replicated, may hold values from -3 to 3
- up_fine: float32 [4, 1536], replicated, may hold values from -4 to 4
- up_coarse: float32 [4, 1536], replicated, may hold values from -4 to 4
- norm_gain: float32 [1536], replicated, may hold values from 0.1 to 1.9
- coarse_qkv: bfloat16 [1536, 2304], P(None, 'sub'), may hold values from -8 to 8
- coarse_out: bfloat16 [768, 1536], P(None, 'sub'), may hold values from -0.21875 to 0.21875
Outputs:
- restored: bfloat16 [65536, 1536], P(('ctx', 'sub'))
The draws below stay inside these ranges and needn't reach their ends.
All inputs are finite; a program needn't handle non-finite values.
Results may differ from the reference program's by a relative error of at most 0.0052.
The reference program's roundings to bfloat16 on the way count: a program that leaves them out, or rounds other values in their place, can miss the bound.
Values may be sent and summed in bfloat16 or wider, within the bound.
A program may use at most 128 MiB of HBM per device.

```python
import math
import jax
import jax.numpy as jnp
from jax import lax

D = 1536
HEADS = 12
HEAD_DIM = 128
CHEADS = 6
SHORT = 4
TOK_DEV = 256
WIN = 1536
CWIDTH = 768
TOKENS = 65536
TOKENS_MID = 16384
TOKENS_TOP = 4096


def shared_keys(key):
    return jnp.clip(jax.random.normal(key, (TOKENS, D), jnp.float32), -6.0, 6.0)


def draw_stream(key, part):
    key = jax.random.fold_in(key, 11)
    key_columns, key_base = jax.random.split(key, 2)
    columns = jnp.exp(jax.random.uniform(key_columns, (1, D), jnp.float32, math.log(0.3), math.log(3.0)))
    base_draw = jnp.clip(jax.random.normal(key_base, (TOKENS, D), jnp.float32), -6.0, 6.0)
    return (base_draw * columns).astype(jnp.bfloat16)


def draw_key_full(key, part):
    base_draw = shared_keys(key)
    return base_draw.astype(jnp.bfloat16)


def draw_query_full(key, part):
    key = jax.random.fold_in(key, 13)
    own_draw = 3.0 * jnp.clip(jax.random.normal(key, (TOKENS, D), jnp.float32), -6.0, 6.0)
    return own_draw.astype(jnp.bfloat16)


def draw_coarse_qkv(key, part):
    key = jax.random.fold_in(key, 14)
    spread = 1.0 / math.sqrt(D)
    drawn_draw = jnp.clip(jax.random.normal(key, (D, 3 * CWIDTH), jnp.float32), -4.0, 4.0) * spread
    queries = 3.0 * drawn_draw[:, :CWIDTH]
    whole = jnp.concatenate([queries, drawn_draw[:, CWIDTH:]], axis=1)
    return jnp.clip(whole, -8.0, 8.0).astype(jnp.bfloat16)


def block_scale(own_key, shape, shards, least, top_value):
    loudness, own = 1.0, jax.random.fold_in(own_key, 6)
    for dim, shards_of in shards:
        draws = jnp.exp(jax.random.uniform(jax.random.fold_in(own, dim), (shards_of,), jnp.float32, least / len(shards), top_value / len(shards)))
        loudness = loudness * jnp.repeat(draws, shape[dim] // shards_of).reshape([-1 if axis == dim else 1 for axis in range(len(shape))])
    return loudness


def gaussian(own_key, shape, deviation, most, cuts=(), kind=jnp.bfloat16):
    loudness = block_scale(own_key, shape, cuts, -0.22, 0.18) if cuts else 1.0
    result = jax.random.normal(own_key, shape, jnp.float32) * deviation * loudness
    return jnp.minimum(jnp.maximum(result, -most), most).astype(kind)


def setup_inputs(seed: int = 0) -> dict:
    key_list = jax.random.split(jax.random.key(seed), 12)
    stream = draw_stream(jax.random.fold_in(key_list[11], 71), 0)
    query_full = draw_query_full(jax.random.fold_in(key_list[11], 71), 0)
    key_full = draw_key_full(jax.random.fold_in(key_list[11], 71), 0)
    value_full = gaussian(key_list[3], (TOKENS, D), 1.0, 6.0, ((0, 256),))
    pool_fine = gaussian(key_list[4], (SHORT, D), 0.5, 3.0, (), jnp.float32)
    pool_coarse = gaussian(key_list[5], (SHORT, D), 0.5, 3.0, (), jnp.float32)
    up_fine = gaussian(key_list[6], (SHORT, D), 0.7, 4.0, (), jnp.float32)
    up_coarse = gaussian(key_list[7], (SHORT, D), 0.7, 4.0, (), jnp.float32)
    norm_gain = jnp.clip(1.0 + 0.18 * jax.random.normal(key_list[8], (D,), jnp.float32), 0.1, 1.9)
    coarse_qkv = draw_coarse_qkv(jax.random.fold_in(key_list[11], 71), 0)
    coarse_out = gaussian(key_list[10], (CWIDTH, D), CWIDTH ** -0.5, 0.21875, ((1, 16),))
    return dict(stream=stream, query_full=query_full, key_full=key_full, value_full=value_full, pool_fine=pool_fine, pool_coarse=pool_coarse, up_fine=up_fine, up_coarse=up_coarse, norm_gain=norm_gain, coarse_qkv=coarse_qkv, coarse_out=coarse_out)


NEGATIVE = -1e+30

def shorten(row_block, weights):
    row_count = row_block.shape[0] // SHORT
    shifted = jnp.concatenate([jnp.zeros((SHORT - 1, row_block.shape[1]), row_block.dtype), row_block[:row_block.shape[0] - (SHORT - 1)]], axis=0)
    grouped = shifted.astype(jnp.float32).reshape(row_count, SHORT, row_block.shape[1])
    return lax.optimization_barrier(jnp.sum(grouped * weights[None, :, :], axis=1)).astype(jnp.bfloat16)

def window_level(stream, query_full, key_full, value_full):
    score_scale = 1.0 / math.sqrt(HEAD_DIM)
    padding = jnp.zeros((WIN, D), jnp.bfloat16)
    keys_all = jnp.concatenate([padding, key_full], axis=0)
    values_all = jnp.concatenate([padding, value_full], axis=0)
    key_span = TOK_DEV + WIN

    def block_output(block_index):
        first_pos = block_index * TOK_DEV
        queries = lax.dynamic_slice_in_dim(query_full, first_pos, TOK_DEV, 0).astype(jnp.float32).reshape(TOK_DEV, HEADS, HEAD_DIM)
        key_rows = lax.dynamic_slice_in_dim(keys_all, first_pos, key_span, 0).astype(jnp.float32).reshape(key_span, HEADS, HEAD_DIM)
        value_rows = lax.dynamic_slice_in_dim(values_all, first_pos, key_span, 0).astype(jnp.float32).reshape(key_span, HEADS, HEAD_DIM)
        base_rows = lax.dynamic_slice_in_dim(stream, first_pos, TOK_DEV, 0).astype(jnp.float32)
        query_pos = first_pos + jnp.arange(TOK_DEV, dtype=jnp.int32)
        key_pos = first_pos - WIN + jnp.arange(key_span, dtype=jnp.int32)
        allowed_mask = (key_pos[None, :] <= query_pos[:, None]) & (key_pos[None, :] > query_pos[:, None] - WIN) & (key_pos[None, :] >= 0)
        scores = jnp.einsum('qhd,khd->hqk', queries, key_rows) * score_scale
        scores = jnp.where(allowed_mask[None], scores, NEGATIVE)
        peak_score = lax.optimization_barrier(jnp.max(scores, axis=2, keepdims=True))
        weights = jnp.where(allowed_mask[None], jnp.exp(scores - peak_score), 0.0)
        total_sum = lax.optimization_barrier(jnp.sum(weights, axis=2))
        rounded = lax.optimization_barrier(weights.astype(jnp.bfloat16)).astype(jnp.float32)
        attended = jnp.einsum('hqk,khd->qhd', rounded, value_rows) / jnp.transpose(total_sum)[:, :, None]
        return (base_rows + attended.reshape(TOK_DEV, D)).astype(jnp.bfloat16)
    blocks = lax.map(block_output, jnp.arange(TOKENS // TOK_DEV, dtype=jnp.int32))
    return blocks.reshape(TOKENS, D)

def coarse_level(summit_rows, norm_gain, coarse_qkv, coarse_out):
    score_scale = 1.0 / math.sqrt(HEAD_DIM)
    summit_wide = summit_rows.astype(jnp.float32)
    normed = (summit_wide * lax.rsqrt(lax.optimization_barrier(jnp.mean(summit_wide * summit_wide, axis=1, keepdims=True)) + 1e-05) * norm_gain).astype(jnp.bfloat16)
    projected = jnp.dot(normed, coarse_qkv, preferred_element_type=jnp.float32).astype(jnp.bfloat16)
    queries = projected[:, :CWIDTH].astype(jnp.float32).reshape(TOKENS_TOP, CHEADS, HEAD_DIM).transpose(1, 0, 2)
    key_rows = projected[:, CWIDTH:2 * CWIDTH].astype(jnp.float32).reshape(TOKENS_TOP, CHEADS, HEAD_DIM).transpose(1, 0, 2)
    value_rows = projected[:, 2 * CWIDTH:].astype(jnp.float32).reshape(TOKENS_TOP, CHEADS, HEAD_DIM).transpose(1, 0, 2)
    position = jnp.arange(TOKENS_TOP, dtype=jnp.int32)
    causal = position[None, :] <= position[:, None]

    def head_output(operands):
        query_one, key_one, value_one = operands
        scores = jnp.dot(query_one, key_one.T, precision=lax.Precision.HIGHEST) * score_scale
        scores = jnp.where(causal, scores, NEGATIVE)
        peak_score = lax.optimization_barrier(jnp.max(scores, axis=1, keepdims=True))
        weights = jnp.where(causal, jnp.exp(scores - peak_score), 0.0)
        total_sum = lax.optimization_barrier(jnp.sum(weights, axis=1, keepdims=True))
        rounded = lax.optimization_barrier(weights.astype(jnp.bfloat16)).astype(jnp.float32)
        return jnp.dot(rounded, value_one, precision=lax.Precision.HIGHEST) / total_sum
    head_results = lax.map(head_output, (queries, key_rows, value_rows))
    attended = head_results.transpose(1, 0, 2).reshape(TOKENS_TOP, CWIDTH).astype(jnp.bfloat16)
    lifted = jnp.dot(attended, coarse_out, preferred_element_type=jnp.float32).astype(jnp.bfloat16)
    return summit_rows.astype(jnp.float32) + lifted.astype(jnp.float32)

def reference(stream, query_full, key_full, value_full, pool_fine, pool_coarse, up_fine, up_coarse, norm_gain, coarse_qkv, coarse_out):
    fine_stream = window_level(stream, query_full, key_full, value_full)
    middle_rows = shorten(fine_stream, pool_fine)
    summit_rows = shorten(middle_rows, pool_coarse)
    summit_sum = coarse_level(summit_rows, norm_gain, coarse_qkv, coarse_out)
    widened = middle_rows.astype(jnp.float32).reshape(TOKENS_TOP, SHORT, D) + up_coarse[None, :, :] * summit_sum[:, None, :]
    widened = widened.reshape(TOKENS_MID, D)
    restored = fine_stream.astype(jnp.float32).reshape(TOKENS_MID, SHORT, D) + up_fine[None, :, :] * widened[:, None, :]
    return restored.reshape(TOKENS, D).astype(jnp.bfloat16)
```

```python
import functools
import math

import jax
import jax.numpy as jnp
from jax import lax
from jax.experimental import pallas as pl
from jax.experimental.pallas import tpu as pltpu
from jax.sharding import PartitionSpec as P

MESH = pl.DeviceIdType.MESH
F32 = jnp.float32
BF16 = jnp.bfloat16

HEADS = 12
CHEADS = 6
HD = 128
SHORT = 4
ROWS = 256
HALF = 128
REACH = 6
CHUNKS = 2 * HEADS
SPAN = 2 * REACH
WIDTH = HEADS * HD
OROWS = HD + 16
LEAD = 24
MROWS = 72
QKV_COLS = 144
OUT_COLS = 96
UNIT = 16
SCALE = math.log2(math.e) / math.sqrt(HD)
NEG = -float(2**100)


def nt(a, b):
    return lax.dot_general(a, b, (((1,), (1,)), ((), ())), preferred_element_type=F32)


def dot(a, b):
    return jnp.dot(a, b, preferred_element_type=F32)


def rounded(x):
    return x.astype(BF16).astype(F32)


def kernel(
    n_ctx, n_sub,
    q_ref, k_ref, v_ref, x_ref, pf_ref, pc_ref, uf_ref, uc_ref, ng_ref, wq_ref, wo_ref,
    out_ref,
    qbuf, oin, oout, vt, fine, ebuf, edge, mid, summit, normed, na, wqs, wos, pt, hb,
    kb, vb, osc, ah, ls, lb,
    q_send, q_recv, o_send, o_recv, e_send, e_recv, w_send, w_recv,
    n_send, n_recv, u_send, u_recv, k_send, k_recv, v_send, v_recv, a_send, a_recv, l_send, l_recv,
):
    ctx = lax.axis_index("ctx")
    sub = lax.axis_index("sub")
    n_all = n_ctx * n_sub
    n_chip = n_sub // 2
    me = ctx * n_sub + sub
    zc = sub // 2
    core = sub % 2
    left = (me + n_all - 1) % n_all
    right = (me + 1) % n_all
    left_id = (left // n_sub, left % n_sub)
    right_id = (right // n_sub, right % n_sub)

    barrier = pltpu.get_barrier_semaphore()

    def greet(device):
        pl.semaphore_signal(barrier, inc=1, device_id=device, device_id_type=MESH)

    greet(left_id)
    greet(right_id)
    for step in range(1, n_sub):
        greet((ctx, (sub + step) % n_sub))
    for step in range(1, n_ctx):
        greet(((ctx + step) % n_ctx, sub))

    for h in range(HEADS):
        vt[h] = v_ref[:, h * HD : (h + 1) * HD].astype(F32).T.astype(BF16)

    pl.semaphore_wait(barrier, 2 + (n_sub - 1) + (n_ctx - 1))

    def remote(src, dst, send, recv, device):
        return pltpu.make_async_remote_copy(
            src_ref=src, dst_ref=dst, send_sem=send, recv_sem=recv,
            device_id=device, device_id_type=MESH,
        )

    sibling = (ctx, 2 * zc)

    def weight_copies():
        return (
            remote(wq_ref, wqs, w_send.at[0], w_recv.at[0], sibling),
            remote(wo_ref, wos, w_send.at[1], w_recv.at[1], sibling),
        )

    @pl.when(core == 1)
    def _():
        for copy in weight_copies():
            copy.start()

    def lanes(h):
        return pl.ds(pl.multiple_of(h * HD, HD), HD)

    def own_rows(half):
        return pl.ds(pl.multiple_of(half * HALF, HALF), HALF)

    def q_copy(s, g):
        if s == 0:
            src = q_ref.at[own_rows(g % 2), lanes(g // 2)]
        else:
            src = qbuf.at[s - 1, g]
        return remote(src, qbuf.at[s, g], q_send.at[s, g % 2], q_recv.at[s, g], left_id)

    def o_copy(s, g):
        return remote(
            oout.at[s - 1, g % 2], oin.at[s - 1, g], o_send.at[s - 1, g % 2], o_recv.at[s - 1, g], right_id
        )

    def edge_copy(h):
        return remote(ebuf.at[:, lanes(h)], edge.at[:, lanes(h)], e_send.at[0], e_recv.at[0], right_id)

    def forward(i, s, g):
        if s > 0:
            q_copy(s - 1, g).wait_recv()

        @pl.when(g >= 2)
        def _():
            q_copy(s, g - 2).wait_send()

        q_copy(s, g).start()

    def partial(s, g):
        h, half = g // 2, g % 2
        keys = k_ref[:, lanes(h)]
        queries = q_ref[own_rows(half), lanes(h)] if s == 0 else qbuf[s - 1, g]
        t = nt(keys, queries) * SCALE
        if s == 0 or s == REACH:
            key_row = lax.broadcasted_iota(jnp.int32, t.shape, 0)
            query_row = lax.broadcasted_iota(jnp.int32, t.shape, 1) + half * HALF
            t = jnp.where(key_row <= query_row if s == 0 else key_row > query_row, t, NEG)
        peak = rounded(jnp.max(t, axis=0, keepdims=True))
        p = jnp.exp2(t - peak)
        total = jnp.sum(p, axis=0, keepdims=True)
        summed = dot(vt[h], p.astype(BF16))
        if s > 0:
            peak = jnp.where(me + s < n_all, peak, NEG)
        return peak, total, summed

    def settle(s, g, state):
        h, half = g // 2, g % 2
        peak, total, summed = state
        if s < REACH:
            o_copy(s + 1, g).wait_recv()
            stats = oin[s, g, HD:OROWS, :].astype(F32)
            before = stats[0:1]
            top = jnp.maximum(before, peak)
            a = jnp.exp2(before - top)
            b = jnp.exp2(peak - top)
            summed = oin[s, g, 0:HD, :].astype(F32) * a + summed * b
            total = (stats[1:2] + stats[2:3]) * a + total * b
            peak = top
        if s > 0:
            slot = g % 2

            @pl.when(g >= 2)
            def _():
                o_copy(s, g - 2).wait_send()

            oout[s - 1, slot, 0:HD, :] = summed.astype(BF16)
            high = rounded(total)
            row = lax.broadcasted_iota(jnp.int32, (16, HALF), 0)
            stats = jnp.where(row == 0, peak, jnp.where(row == 1, high, total - high))
            oout[s - 1, slot, HD:OROWS, :] = stats.astype(BF16)
            o_copy(s, g).start()
        else:
            attended = (summed / total).T
            base = x_ref[own_rows(half), lanes(h)].astype(F32)
            rows16 = (base + attended).astype(BF16)
            fine[h, pl.ds(pl.multiple_of(LEAD + half * HALF, 8), HALF), :] = rows16.astype(F32)

            @pl.when(half == 1)
            def _():
                ebuf[:, lanes(h)] = rows16[HALF - 16 :, :]
                edge_copy(h).start()

    def guarded(i, steps_q, steps_o):
        for s in steps_q:
            g = i - s

            @pl.when((g >= 0) & (g < CHUNKS))
            def _(s=s, g=g):
                forward(i, s, g)

        for s in steps_o:
            g = i - SPAN + s

            @pl.when((g >= 0) & (g < CHUNKS))
            def _(s=s, g=g):
                if s == REACH:
                    q_copy(s - 1, g).wait_recv()
                settle(s, g, partial(s, g))

    def ramp_up(i, carry):
        guarded(i, range(REACH), range(REACH, -1, -1))
        return carry

    def steady(i, carry):
        for s in range(REACH):
            g = i - s

            @pl.when(g < CHUNKS)
            def _(s=s, g=g):
                forward(i, s, g)

        q_copy(REACH - 1, i - REACH).wait_recv()
        states = {s: partial(s, i - SPAN + s) for s in range(REACH, -1, -1)}
        for s in range(REACH, -1, -1):
            settle(s, i - SPAN + s, states[s])
        return carry

    def ramp_down(i, carry):
        guarded(i, (), range(REACH - 1, -1, -1))
        return carry

    lax.fori_loop(0, SPAN, ramp_up, 0)
    lax.fori_loop(SPAN, CHUNKS + REACH, steady, 0)
    lax.fori_loop(CHUNKS + REACH, CHUNKS + SPAN, ramp_down, 0)

    for s in range(REACH):
        for slot in range(2):
            q_copy(s, CHUNKS - 2 + slot).wait_send()
            o_copy(s + 1, CHUNKS - 2 + slot).wait_send()

    whole_edge = remote(ebuf, edge, e_send.at[0], e_recv.at[0], right_id)
    whole_edge.wait_recv()
    square = jnp.zeros((16, 1), F32)
    for h in range(HEADS):
        at = slice(h * HD, (h + 1) * HD)
        fine[h, 0:8, :] = jnp.zeros((8, HD), F32)
        fine[h, 8:LEAD, :] = jnp.where(me > 0, edge[:, at].astype(F32), 0.0)
        row = jnp.zeros((68, HD), F32)
        for k in range(SHORT):
            row = row + fine[h, pl.ds(LEAD - 19 + k, 68, stride=SHORT), :] * pf_ref[k : k + 1, at]
        mid[h, 0:68, :] = rounded(row)
        row = jnp.zeros((16, HD), F32)
        for k in range(SHORT):
            row = row + mid[h, pl.ds(1 + k, 16, stride=SHORT), :] * pc_ref[k : k + 1, at]
        row = rounded(row)
        summit[:, at] = row
        square = square + jnp.sum(row * row, axis=1, keepdims=True)
    whole_edge.wait_send()
    normed[...] = (summit[...] * lax.rsqrt(square / WIDTH + 1e-05) * ng_ref[...]).astype(BF16)

    def n_copy(step):
        target = (zc + step) % n_chip
        return remote(normed, na.at[sub], n_send.at[step], n_recv.at[sub], (ctx, 2 * target))

    def n_arrival(source):
        return remote(normed, na.at[source], n_send.at[0], n_recv.at[source], sibling)

    for step in range(1, n_chip):
        n_copy(step).start()

    @pl.when(core == 1)
    def _():
        n_copy(0).start()

    def u_copy(i, head, dest):
        unit = 18 * zc + i
        piece = unit // 8
        at = pl.multiple_of((piece // CHEADS) * HD + (unit % 8) * UNIT, UNIT)
        return pt.at[pl.ds(i * UNIT, UNIT)], hb.at[pl.ds(at, UNIT)]

    def spread(i):
        unit = 18 * zc + i
        piece = unit // 8
        head = piece % CHEADS
        src, dst = u_copy(i, head, None)
        return head, remote(src, dst, u_send.at[i], u_recv.at[0], (ctx, 2 * head)), pltpu.make_async_copy(src, dst, u_recv.at[0])

    def k_copy(source, step):
        return remote(kb.at[source], kb.at[source], k_send.at[step], k_recv.at[source], (source + step, sub))

    def v_copy(source, step):
        return remote(vb.at[source], vb.at[source], v_send.at[step], v_recv.at[source], (source + step, sub))

    def a_copy(step):
        return remote(ah.at[zc], ah.at[zc], a_send.at[step], a_recv.at[zc], (ctx, 2 * ((zc + step) % n_chip)))

    def l_copy(step):
        target = (sub + step) % n_sub
        rows = pl.ds(pl.multiple_of(target * UNIT, UNIT), UNIT)
        return remote(ls.at[:, rows, :], lb.at[zc], l_send.at[step], l_recv.at[zc], (ctx, target))

    @pl.when(core == 0)
    def _():
        na[sub] = normed[...]
        for copy in weight_copies():
            copy.wait_recv()
        for source in range(n_sub):
            @pl.when(source != sub)
            def _(source=source):
                n_arrival(source).wait_recv()
        rows = na[...].reshape(ROWS, WIDTH)
        pad = jnp.zeros((ROWS, ROWS - QKV_COLS), F32)
        for place, w in enumerate((wq_ref, wqs)):
            wide = jnp.concatenate([dot(rows, w[...]), pad], axis=1).T
            pt[place * QKV_COLS : (place + 1) * QKV_COLS, :] = wide[:QKV_COLS].astype(BF16)
        for i in range(18):
            head, away, here = spread(i)

            @pl.when(head == zc)
            def _(here=here):
                here.start()

            @pl.when(head != zc)
            def _(away=away):
                away.start()

    @pl.when((core == 0) & (zc < CHEADS))
    def _():
        pltpu.make_async_copy(hb, hb, u_recv.at[0]).wait()
        queries = hb[0:HD].astype(F32).T.astype(BF16)
        kb[ctx] = hb[HD : 2 * HD].astype(F32).T.astype(BF16)
        vb[ctx] = hb[2 * HD : 3 * HD]
        for step in range(1, n_ctx):
            @pl.when(ctx + step < n_ctx)
            def _(step=step):
                k_copy(ctx, step).start()
                v_copy(ctx, step).start()

        t = nt(kb[ctx], queries) * SCALE
        key_row = lax.broadcasted_iota(jnp.int32, t.shape, 0)
        query_row = lax.broadcasted_iota(jnp.int32, t.shape, 1)
        t = jnp.where(key_row <= query_row, t, NEG)
        peak = jnp.max(t, axis=0, keepdims=True)
        p = jnp.exp2(t - peak)
        total = jnp.sum(p, axis=0, keepdims=True)
        osc[...] = dot(vb[ctx], p.astype(BF16))

        def fold(i, carry):
            before, total = carry
            source = ctx - 1 - i
            k_copy(source, 1).wait_recv()
            v_copy(source, 1).wait_recv()
            t = nt(kb[source], queries) * SCALE
            peak = jnp.maximum(before, jnp.max(t, axis=0, keepdims=True))
            p = jnp.exp2(t - peak)
            a = jnp.exp2(before - peak)
            osc[...] = osc[...] * a + dot(vb[source], p.astype(BF16))
            return peak, total * a + jnp.sum(p, axis=0, keepdims=True)

        peak, total = lax.fori_loop(0, ctx, fold, (peak, total))
        ah[zc] = (osc[...] / total).T.astype(BF16)
        for step in range(1, n_chip):
            a_copy(step).start()

    @pl.when(core == 0)
    def _():
        for head in range(CHEADS):
            @pl.when(head != zc)
            def _(head=head):
                remote(ah.at[head], ah.at[head], a_send.at[0], a_recv.at[head], sibling).wait_recv()
        pad = jnp.zeros((ROWS, HD - OUT_COLS), F32)
        for place, w in enumerate((wo_ref, wos)):
            lifted = dot(ah[0], w[0:HD, :])
            for head in range(1, CHEADS):
                lifted = lifted + dot(ah[head], w[head * HD : (head + 1) * HD, :])
            ls[place] = jnp.concatenate([lifted, pad], axis=1).astype(BF16)
        for step in range(1, n_sub):
            l_copy(step).start()
        lb[zc] = ls[:, pl.ds(pl.multiple_of(sub * UNIT, UNIT), UNIT), :]

    for chip in range(n_chip):
        @pl.when((core == 1) | (chip != zc))
        def _(chip=chip):
            remote(ls.at[:, 0:UNIT, :], lb.at[chip], l_send.at[0], l_recv.at[chip], sibling).wait_recv()

    pieces = []
    for chip in range(n_chip):
        for place in range(2):
            pieces.append(lb[chip, place].astype(F32)[:, :OUT_COLS])
    summit[...] = summit[...] + jnp.concatenate(pieces, axis=1)

    for h in range(HEADS):
        at = slice(h * HD, (h + 1) * HD)
        lift = summit[:, at]
        for k in range(SHORT):
            place = pl.ds(4 + k, 16, stride=SHORT)
            mid[h, place, :] = mid[h, place, :] + uc_ref[k : k + 1, at] * lift
        lift = mid[h, 4:68, :]
        for k in range(SHORT):
            place = pl.ds(LEAD + k, 64, stride=SHORT)
            fine[h, place, :] = fine[h, place, :] + uf_ref[k : k + 1, at] * lift
        out_ref[:, at] = fine[h, LEAD : LEAD + ROWS, :].astype(BF16)

    whole_edge_done = None
    @pl.when(core == 1)
    def _():
        for copy in weight_copies():
            copy.wait_send()
        n_copy(0).wait_send()

    for step in range(1, n_chip):
        n_copy(step).wait_send()

    @pl.when(core == 0)
    def _():
        for i in range(18):
            head, away, here = spread(i)

            @pl.when(head != zc)
            def _(away=away):
                away.wait_send()
        for step in range(1, n_sub):
            l_copy(step).wait_send()

    @pl.when((core == 0) & (zc < CHEADS))
    def _():
        for step in range(1, n_ctx):
            @pl.when(ctx + step < n_ctx)
            def _(step=step):
                k_copy(ctx, step).wait_send()
                v_copy(ctx, step).wait_send()
        for step in range(1, n_chip):
            a_copy(step).wait_send()


def solution(mesh):
    n_ctx, n_sub = mesh.shape["ctx"], mesh.shape["sub"]
    n_chip = n_sub // 2
    dma = pltpu.SemaphoreType.DMA

    def shards(stream, q, k, v, pf, pc, uf, uc, ng, wq, wo):
        vmem = pl.BlockSpec(memory_space=pltpu.VMEM)
        return pl.pallas_call(
            functools.partial(kernel, n_ctx, n_sub),
            out_shape=jax.ShapeDtypeStruct((ROWS, WIDTH), BF16),
            in_specs=[vmem] * 11,
            out_specs=vmem,
            scratch_shapes=[
                pltpu.VMEM((REACH, CHUNKS, HALF, HD), BF16),
                pltpu.VMEM((REACH, CHUNKS, OROWS, HALF), BF16),
                pltpu.VMEM((REACH, 2, OROWS, HALF), BF16),
                pltpu.VMEM((HEADS, HD, ROWS), BF16),
                pltpu.VMEM((HEADS, LEAD + ROWS, HD), F32),
                pltpu.VMEM((16, WIDTH), BF16),
                pltpu.VMEM((16, WIDTH), BF16),
                pltpu.VMEM((HEADS, MROWS, HD), F32),
                pltpu.VMEM((16, WIDTH), F32),
                pltpu.VMEM((16, WIDTH), BF16),
                pltpu.VMEM((n_sub, 16, WIDTH), BF16),
                pltpu.VMEM(wq.shape, BF16),
                pltpu.VMEM(wo.shape, BF16),
                pltpu.VMEM((2 * QKV_COLS, ROWS), BF16),
                pltpu.VMEM((3 * HD, ROWS), BF16),
                pltpu.VMEM((n_ctx, ROWS, HD), BF16),
                pltpu.VMEM((n_ctx, HD, ROWS), BF16),
                pltpu.VMEM((HD, ROWS), F32),
                pltpu.VMEM((CHEADS, ROWS, HD), BF16),
                pltpu.VMEM((2, ROWS, HD), BF16),
                pltpu.VMEM((n_chip, 2, UNIT, HD), BF16),
                dma((REACH, 2)), dma((REACH, CHUNKS)),
                dma((REACH, 2)), dma((REACH, CHUNKS)),
                dma((1,)), dma((1,)),
                dma((2,)), dma((2,)),
                dma((n_chip,)), dma((n_sub,)),
                dma((18,)), dma((1,)),
                dma((n_ctx,)), dma((n_ctx,)),
                dma((n_ctx,)), dma((n_ctx,)),
                dma((n_chip,)), dma((CHEADS,)),
                dma((n_sub,)), dma((n_chip,)),
            ],
            compiler_params=pltpu.CompilerParams(
                collective_id=0, has_side_effects=True, vmem_limit_bytes=60 * 2**20
            ),
        )(q, k, v, stream, pf, pc, uf, uc, ng.reshape(1, WIDTH), wq, wo)

    rows = P(("ctx", "sub"), None)
    return jax.shard_map(
        shards,
        mesh=mesh,
        in_specs=(rows, rows, rows, rows, P(), P(), P(), P(), P(), P(None, "sub"), P(None, "sub")),
        out_specs=rows,
        check_vma=False,
    )
```

```python
import functools
import math

import jax
import jax.numpy as jnp
from jax import lax
from jax.experimental import pallas as pl
from jax.experimental.pallas import tpu as pltpu
from jax.sharding import PartitionSpec as P

MESH = pl.DeviceIdType.MESH
F32 = jnp.float32
BF16 = jnp.bfloat16

HEADS = 12
CHEADS = 6
HD = 128
SHORT = 4
ROWS = 256
CHIP_ROWS = 2 * ROWS
OWN = HEADS // 2
HALF = 128
BLOCKS = CHIP_ROWS // HALF
REACH = 3
CHUNKS = OWN * BLOCKS
LAG = 2
SLOTS = 4
SPAN = 2 * REACH * LAG
WIDTH = HEADS * HD
OROWS = HD + 16
LEAD = 24
MROWS = 72
QKV_COLS = 144
OUT_COLS = 96
UNIT = 16
SCALE = math.log2(math.e) / math.sqrt(HD)
NEG = -float(2**100)


def nt(a, b):
    return lax.dot_general(a, b, (((1,), (1,)), ((), ())), preferred_element_type=F32)


def dot(a, b):
    return jnp.dot(a, b, preferred_element_type=F32)


def rounded(x):
    return x.astype(BF16).astype(F32)


def kernel(
    n_ctx, n_sub,
    q_ref, k_ref, v_ref, x_ref, pf_ref, pc_ref, uf_ref, uc_ref, ng_ref, wq_ref, wo_ref,
    out_ref,
    qx, kx, vx, xx, qbuf, oin, oout, vt, fout, fine, mid, summit, normed, na, wqs, wos, pt, hb,
    kb, vb, osc, ah, ls, lb,
    x_send, x_recv, q_send, q_recv, o_send, o_recv, f_send, f_recv, e_send, e_recv, w_send, w_recv,
    n_send, n_recv, u_send, u_recv, k_send, k_recv, v_send, v_recv, a_send, a_recv, l_send, l_recv,
):
    ctx = lax.axis_index("ctx")
    sub = lax.axis_index("sub")
    n_chip = n_sub // 2
    n_chips = n_ctx * n_chip
    me = ctx * n_sub + sub
    zc = sub // 2
    core = sub % 2
    other = 1 - core
    chip = ctx * n_chip + zc
    left = (chip + n_chips - 1) % n_chips
    right = (chip + 1) % n_chips
    left_id = (left // n_chip, 2 * (left % n_chip) + core)
    right_id = (right // n_chip, 2 * (right % n_chip) + core)
    right_first = (right // n_chip, 2 * (right % n_chip))
    twin = (ctx, 2 * zc + other)

    barrier = pltpu.get_barrier_semaphore()

    def greet(device):
        pl.semaphore_signal(barrier, inc=1, device_id=device, device_id_type=MESH)

    for near in (left, right):
        for side in range(2):
            greet((near // n_chip, 2 * (near % n_chip) + side))
    for step in range(1, n_sub):
        greet((ctx, (sub + step) % n_sub))
    for step in range(1, n_ctx):
        greet(((ctx + step) % n_ctx, sub))

    def remote(src, dst, send, recv, device):
        return pltpu.make_async_remote_copy(
            src_ref=src, dst_ref=dst, send_sem=send, recv_sem=recv,
            device_id=device, device_id_type=MESH,
        )

    own_rows = pl.ds(pl.multiple_of(core * ROWS, ROWS), ROWS)
    own_lanes = pl.ds(pl.multiple_of(core * OWN * HD, HD), OWN * HD)
    twin_lanes = pl.ds(pl.multiple_of(other * OWN * HD, HD), OWN * HD)
    parts = ((q_ref, qx), (k_ref, kx), (v_ref, vx), (x_ref, xx))
    for src, dst in parts:
        dst[own_rows, :] = src[:, own_lanes]

    def halves(n):
        src, dst = parts[n]
        return remote(src.at[:, twin_lanes], dst.at[own_rows], x_send.at[n], x_recv.at[n], twin)

    pl.semaphore_wait(barrier, 4 + (n_sub - 1) + (n_ctx - 1))
    for n in range(4):
        halves(n).start()

    sibling = (ctx, 2 * zc)

    def weight_copies():
        return (
            remote(wq_ref, wqs, w_send.at[0], w_recv.at[0], sibling),
            remote(wo_ref, wos, w_send.at[1], w_recv.at[1], sibling),
        )

    @pl.when(core == 1)
    def _():
        for copy in weight_copies():
            copy.start()

    def lanes(h):
        return pl.ds(pl.multiple_of(h * HD, HD), HD)

    def place(g):
        return g // BLOCKS, (g + 2 * core) % BLOCKS

    def block_rows(block):
        return pl.ds(pl.multiple_of(block * HALF, HALF), HALF)

    def q_copy(s, g):
        if s == 0:
            h, block = place(g)
            src = qx.at[block_rows(block), lanes(h)]
        else:
            src = qbuf.at[s - 1, g]
        return remote(src, qbuf.at[s, g], q_send.at[s, g % SLOTS], q_recv.at[s, g], left_id)

    def o_copy(s, g):
        return remote(
            oout.at[s - 1, g % SLOTS], oin.at[s - 1, g], o_send.at[s - 1, g % SLOTS],
            o_recv.at[s - 1, g], right_id,
        )

    def f_copy(h, half):
        head = core * OWN + h
        rows = pl.ds(pl.multiple_of(LEAD + half * HALF, 8), HALF)
        return remote(fout.at[h, half], fine.at[head, rows, :], f_send.at[h, half], f_recv.at[0], twin)

    def edge_of(h, device, slot):
        head = core * OWN + h
        return remote(
            fout.at[h, 2 + slot, pl.ds(HALF - 16, 16), :], fine.at[head, pl.ds(8, 16), :],
            e_send.at[h, slot], e_recv.at[0], device,
        )

    def forward(s, g):
        if s > 0:
            q_copy(s - 1, g).wait_recv()

        @pl.when(g >= SLOTS)
        def _():
            q_copy(s, g - SLOTS).wait_send()

        q_copy(s, g).start()

    def partial(s, g):
        h, block = place(g)
        keys = kx[:, lanes(h)]
        queries = qx[block_rows(block), lanes(h)] if s == 0 else qbuf[s - 1, g]
        t = nt(keys, queries) * SCALE
        if s == 0 or s == REACH:
            key_row = lax.broadcasted_iota(jnp.int32, t.shape, 0)
            query_row = lax.broadcasted_iota(jnp.int32, t.shape, 1) + block * HALF
            t = jnp.where(key_row <= query_row if s == 0 else key_row > query_row, t, NEG)
        peak = rounded(jnp.max(t, axis=0, keepdims=True))
        p = jnp.exp2(t - peak)
        total = jnp.sum(p, axis=0, keepdims=True)
        summed = dot(vt[h], p.astype(BF16))
        if s > 0:
            peak = jnp.where(chip + s < n_chips, peak, NEG)
        return peak, total, summed

    def settle(s, g, state):
        h, block = place(g)
        peak, total, summed = state
        if s < REACH:
            o_copy(s + 1, g).wait_recv()
            stats = oin[s, g, HD:OROWS, :].astype(F32)
            before = stats[0:1]
            top = jnp.maximum(before, peak)
            a = jnp.exp2(before - top)
            b = jnp.exp2(peak - top)
            summed = oin[s, g, 0:HD, :].astype(F32) * a + summed * b
            total = (stats[1:2] + stats[2:3]) * a + total * b
            peak = top
        if s > 0:
            slot = g % SLOTS

            @pl.when(g >= SLOTS)
            def _():
                o_copy(s, g - SLOTS).wait_send()

            oout[s - 1, slot, 0:HD, :] = summed.astype(BF16)
            high = rounded(total)
            row = lax.broadcasted_iota(jnp.int32, (16, HALF), 0)
            stats = jnp.where(row == 0, peak, jnp.where(row == 1, high, total - high))
            oout[s - 1, slot, HD:OROWS, :] = stats.astype(BF16)
            o_copy(s, g).start()
        else:
            attended = (summed / total).T
            base = xx[block_rows(block), lanes(h)].astype(F32)
            rows = rounded(base + attended)
            head = core * OWN + h
            half = block % 2

            @pl.when(block // 2 == core)
            def _():
                fine[head, pl.ds(pl.multiple_of(LEAD + half * HALF, 8), HALF), :] = rows

            @pl.when(block // 2 != core)
            def _():
                fout[h, half] = rows
                f_copy(h, half).start()

            @pl.when((block == 1) & (core == 1))
            def _():
                fine[head, 8:LEAD, :] = rows[HALF - 16 :, :]

            @pl.when((block == 1) & (core == 0))
            def _():
                fout[h, 2] = rows
                edge_of(h, twin, 0).start()

            @pl.when(block == 3)
            def _():
                fout[h, 3] = rows
                edge_of(h, right_first, 1).start()

    def guarded(i, steps_q, steps_o):
        for s in steps_q:
            g = i - s * LAG

            @pl.when((g >= 0) & (g < CHUNKS))
            def _(s=s, g=g):
                forward(s, g)

        for s in steps_o:
            g = i - (2 * REACH - s) * LAG

            @pl.when((g >= 0) & (g < CHUNKS))
            def _(s=s, g=g):
                if s == REACH:
                    q_copy(s - 1, g).wait_recv()
                settle(s, g, partial(s, g))

    def first(i, carry):
        guarded(i, range(REACH), ())
        return carry

    def ramp_up(i, carry):
        guarded(i, range(REACH), range(REACH, -1, -1))
        return carry

    def steady(i, carry):
        for s in range(REACH):
            g = i - s * LAG

            @pl.when(g < CHUNKS)
            def _(s=s, g=g):
                forward(s, g)

        at = {s: i - (2 * REACH - s) * LAG for s in range(REACH + 1)}
        q_copy(REACH - 1, at[REACH]).wait_recv()
        states = {s: partial(s, at[s]) for s in range(REACH, -1, -1)}
        for s in range(REACH, -1, -1):
            settle(s, at[s], states[s])
        return carry

    def ramp_down(i, carry):
        guarded(i, (), range(REACH - 1, -1, -1))
        return carry

    halves(0).wait_recv()
    lax.fori_loop(0, REACH, first, 0)
    halves(2).wait_recv()
    for h in range(OWN):
        vt[h] = vx[:, h * HD : (h + 1) * HD].astype(F32).T.astype(BF16)
    halves(1).wait_recv()
    halves(3).wait_recv()
    lax.fori_loop(REACH, SPAN, ramp_up, 0)
    lax.fori_loop(SPAN, CHUNKS + REACH * LAG, steady, 0)
    lax.fori_loop(CHUNKS + REACH * LAG, CHUNKS + SPAN, ramp_down, 0)

    theirs = fine.at[pl.ds(other * OWN, OWN), pl.ds(LEAD, ROWS), :]
    pltpu.make_async_copy(theirs, theirs, f_recv.at[0]).wait()

    @pl.when(core == 0)
    def _():
        rim = fine.at[:, pl.ds(8, 16), :]
        pltpu.make_async_copy(rim, rim, e_recv.at[0]).wait()

    @pl.when(core == 1)
    def _():
        rim = fine.at[pl.ds(0, OWN), pl.ds(8, 16), :]
        pltpu.make_async_copy(rim, rim, e_recv.at[0]).wait()

    square = jnp.zeros((16, 1), F32)
    for h in range(HEADS):
        at = slice(h * HD, (h + 1) * HD)
        fine[h, 0:8, :] = jnp.zeros((8, HD), F32)
        fine[h, 8:LEAD, :] = jnp.where(me > 0, fine[h, 8:LEAD, :], 0.0)
        row = jnp.zeros((68, HD), F32)
        for k in range(SHORT):
            row = row + fine[h, pl.ds(LEAD - 19 + k, 68, stride=SHORT), :] * pf_ref[k : k + 1, at]
        mid[h, 0:68, :] = rounded(row)
        row = jnp.zeros((16, HD), F32)
        for k in range(SHORT):
            row = row + mid[h, pl.ds(1 + k, 16, stride=SHORT), :] * pc_ref[k : k + 1, at]
        row = rounded(row)
        summit[:, at] = row
        square = square + jnp.sum(row * row, axis=1, keepdims=True)
    normed[...] = (summit[...] * lax.rsqrt(square / WIDTH + 1e-05) * ng_ref[...].reshape(1, WIDTH)).astype(BF16)

    def n_copy(step):
        target = (zc + step) % n_chip
        return remote(normed, na.at[sub], n_send.at[step], n_recv.at[sub], (ctx, 2 * target))

    def n_arrival(source):
        return remote(normed, na.at[source], n_send.at[0], n_recv.at[source], sibling)

    for step in range(1, n_chip):
        n_copy(step).start()

    @pl.when(core == 1)
    def _():
        n_copy(0).start()

    def spread(i):
        unit = 18 * zc + i
        piece = unit // 8
        head = piece % CHEADS
        at = pl.multiple_of((piece // CHEADS) * HD + (unit % 8) * UNIT, UNIT)
        src, dst = pt.at[pl.ds(i * UNIT, UNIT)], hb.at[pl.ds(at, UNIT)]
        return (
            head,
            lambda: remote(src, dst, u_send.at[i], u_recv.at[0], (ctx, 2 * head)),
            lambda: pltpu.make_async_copy(src, dst, u_recv.at[0]),
        )

    def k_copy(source, step):
        return remote(kb.at[source], kb.at[source], k_send.at[step], k_recv.at[source], (source + step, sub))

    def v_copy(source, step):
        return remote(vb.at[source], vb.at[source], v_send.at[step], v_recv.at[source], (source + step, sub))

    def a_copy(step):
        return remote(ah.at[zc], ah.at[zc], a_send.at[step], a_recv.at[zc], (ctx, 2 * ((zc + step) % n_chip)))

    def l_copy(step):
        target = (sub + step) % n_sub
        rows = pl.ds(pl.multiple_of(target * UNIT, UNIT), UNIT)
        return remote(ls.at[:, rows, :], lb.at[zc], l_send.at[step], l_recv.at[zc], (ctx, target))

    @pl.when(core == 0)
    def _():
        na[sub] = normed[...]
        for copy in weight_copies():
            copy.wait_recv()
        for source in range(n_sub):
            @pl.when(source != sub)
            def _(source=source):
                n_arrival(source).wait_recv()
        rows = na[...].reshape(ROWS, WIDTH)
        for turn, w in enumerate((wq_ref, wqs)):
            pt[turn * QKV_COLS : (turn + 1) * QKV_COLS, :] = nt(w[...], rows).astype(BF16)
        for i in range(18):
            head, away, here = spread(i)

            @pl.when(head == zc)
            def _(here=here):
                here().start()

            @pl.when(head != zc)
            def _(away=away):
                away().start()

    @pl.when((core == 0) & (zc < CHEADS))
    def _():
        pltpu.make_async_copy(hb, hb, u_recv.at[0]).wait()
        queries = hb[0:HD].astype(F32).T.astype(BF16)
        kb[ctx] = hb[HD : 2 * HD].astype(F32).T.astype(BF16)
        vb[ctx] = hb[2 * HD : 3 * HD]
        for step in range(1, n_ctx):
            @pl.when(ctx + step < n_ctx)
            def _(step=step):
                k_copy(ctx, step).start()
                v_copy(ctx, step).start()

        t = nt(kb[ctx], queries) * SCALE
        key_row = lax.broadcasted_iota(jnp.int32, t.shape, 0)
        query_row = lax.broadcasted_iota(jnp.int32, t.shape, 1)
        t = jnp.where(key_row <= query_row, t, NEG)
        peak = jnp.max(t, axis=0, keepdims=True)
        p = jnp.exp2(t - peak)
        total = jnp.sum(p, axis=0, keepdims=True)
        osc[...] = dot(vb[ctx], p.astype(BF16))

        def fold(i, carry):
            before, total = carry
            source = ctx - 1 - i
            k_copy(source, 1).wait_recv()
            v_copy(source, 1).wait_recv()
            t = nt(kb[source], queries) * SCALE
            peak = jnp.maximum(before, jnp.max(t, axis=0, keepdims=True))
            p = jnp.exp2(t - peak)
            a = jnp.exp2(before - peak)
            osc[...] = osc[...] * a + dot(vb[source], p.astype(BF16))
            return peak, total * a + jnp.sum(p, axis=0, keepdims=True)

        peak, total = lax.fori_loop(0, ctx, fold, (peak, total))
        ah[zc] = (osc[...] / total).T.astype(BF16)
        for step in range(1, n_chip):
            a_copy(step).start()

    @pl.when(core == 0)
    def _():
        for head in range(CHEADS):
            @pl.when(head != zc)
            def _(head=head):
                remote(ah.at[head], ah.at[head], a_send.at[0], a_recv.at[head], sibling).wait_recv()
        pad = jnp.zeros((ROWS, HD - OUT_COLS), F32)
        for turn, w in enumerate((wo_ref, wos)):
            lifted = nt(ah[0], w[:, 0:HD])
            for head in range(1, CHEADS):
                lifted = lifted + nt(ah[head], w[:, head * HD : (head + 1) * HD])
            ls[turn] = jnp.concatenate([lifted, pad], axis=1).astype(BF16)
        for step in range(1, n_sub):
            l_copy(step).start()
        lb[zc] = ls[:, pl.ds(pl.multiple_of(sub * UNIT, UNIT), UNIT), :]

    for source in range(n_chip):
        @pl.when((core == 1) | (source != zc))
        def _(source=source):
            remote(ls.at[:, 0:UNIT, :], lb.at[source], l_send.at[0], l_recv.at[source], sibling).wait_recv()

    pieces = []
    for source in range(n_chip):
        for turn in range(2):
            pieces.append(lb[source, turn].astype(F32)[:, :OUT_COLS])
    summit[...] = summit[...] + jnp.concatenate(pieces, axis=1)

    for h in range(HEADS):
        at = slice(h * HD, (h + 1) * HD)
        lift = summit[:, at]
        for k in range(SHORT):
            spots = pl.ds(4 + k, 16, stride=SHORT)
            mid[h, spots, :] = mid[h, spots, :] + uc_ref[k : k + 1, at] * lift
        lift = mid[h, 4:68, :]
        for k in range(SHORT):
            spots = pl.ds(LEAD + k, 64, stride=SHORT)
            fine[h, spots, :] = fine[h, spots, :] + uf_ref[k : k + 1, at] * lift
        out_ref[:, at] = fine[h, LEAD : LEAD + ROWS, :].astype(BF16)

    for n in range(4):
        halves(n).wait_send()
    for s in range(REACH):
        for slot in range(SLOTS):
            q_copy(s, CHUNKS - SLOTS + slot).wait_send()
            o_copy(s + 1, CHUNKS - SLOTS + slot).wait_send()
    for h in range(OWN):
        for half in range(2):
            f_copy(h, half).wait_send()
        edge_of(h, right_first, 1).wait_send()

        @pl.when(core == 0)
        def _(h=h):
            edge_of(h, twin, 0).wait_send()

    @pl.when(core == 1)
    def _():
        for copy in weight_copies():
            copy.wait_send()
        n_copy(0).wait_send()

    for step in range(1, n_chip):
        n_copy(step).wait_send()

    @pl.when(core == 0)
    def _():
        for i in range(18):
            head, away, here = spread(i)

            @pl.when(head != zc)
            def _(away=away):
                away().wait_send()
        for step in range(1, n_sub):
            l_copy(step).wait_send()

    @pl.when((core == 0) & (zc < CHEADS))
    def _():
        for step in range(1, n_ctx):
            @pl.when(ctx + step < n_ctx)
            def _(step=step):
                k_copy(ctx, step).wait_send()
                v_copy(ctx, step).wait_send()
        for step in range(1, n_chip):
            a_copy(step).wait_send()


def solution(mesh):
    n_ctx, n_sub = mesh.shape["ctx"], mesh.shape["sub"]
    n_chip = n_sub // 2
    dma = pltpu.SemaphoreType.DMA

    def shards(stream, q, k, v, pf, pc, uf, uc, ng, wq, wo):
        vmem = pl.BlockSpec(memory_space=pltpu.VMEM)
        return pl.pallas_call(
            functools.partial(kernel, n_ctx, n_sub),
            out_shape=jax.ShapeDtypeStruct((ROWS, WIDTH), BF16),
            in_specs=[vmem] * 11,
            out_specs=vmem,
            scratch_shapes=[
                *[pltpu.VMEM((CHIP_ROWS, OWN * HD), BF16)] * 4,
                pltpu.VMEM((REACH, CHUNKS, HALF, HD), BF16),
                pltpu.VMEM((REACH, CHUNKS, OROWS, HALF), BF16),
                pltpu.VMEM((REACH, SLOTS, OROWS, HALF), BF16),
                pltpu.VMEM((OWN, HD, CHIP_ROWS), BF16),
                pltpu.VMEM((OWN, 4, HALF, HD), F32),
                pltpu.VMEM((HEADS, LEAD + ROWS, HD), F32),
                pltpu.VMEM((HEADS, MROWS, HD), F32),
                pltpu.VMEM((16, WIDTH), F32),
                pltpu.VMEM((16, WIDTH), BF16),
                pltpu.VMEM((n_sub, 16, WIDTH), BF16),
                pltpu.VMEM((QKV_COLS, WIDTH), BF16),
                pltpu.VMEM((OUT_COLS, CHEADS * HD), BF16),
                pltpu.VMEM((2 * QKV_COLS, ROWS), BF16),
                pltpu.VMEM((3 * HD, ROWS), BF16),
                pltpu.VMEM((n_ctx, ROWS, HD), BF16),
                pltpu.VMEM((n_ctx, HD, ROWS), BF16),
                pltpu.VMEM((HD, ROWS), F32),
                pltpu.VMEM((CHEADS, ROWS, HD), BF16),
                pltpu.VMEM((2, ROWS, HD), BF16),
                pltpu.VMEM((n_chip, 2, UNIT, HD), BF16),
                dma((4,)), dma((4,)),
                dma((REACH, SLOTS)), dma((REACH, CHUNKS)),
                dma((REACH, SLOTS)), dma((REACH, CHUNKS)),
                dma((OWN, 2)), dma((1,)),
                dma((OWN, 2)), dma((1,)),
                dma((2,)), dma((2,)),
                dma((n_chip,)), dma((n_sub,)),
                dma((18,)), dma((1,)),
                dma((n_ctx,)), dma((n_ctx,)),
                dma((n_ctx,)), dma((n_ctx,)),
                dma((n_chip,)), dma((CHEADS,)),
                dma((n_sub,)), dma((n_chip,)),
            ],
            compiler_params=pltpu.CompilerParams(
                collective_id=0, has_side_effects=True, vmem_limit_bytes=60 * 2**20
            ),
        )(q, k, v, stream, pf, pc, uf, uc, ng, wq.T, wo.T)

    rows = P(("ctx", "sub"), None)
    return jax.shard_map(
        shards,
        mesh=mesh,
        in_specs=(rows, rows, rows, rows, P(), P(), P(), P(), P(), P(None, "sub"), P(None, "sub")),
        out_specs=rows,
        check_vma=False,
    )
```

```python
import functools
import math

import jax
import jax.numpy as jnp
from jax import lax
from jax.experimental import pallas as pl
from jax.experimental.pallas import tpu as pltpu
from jax.sharding import PartitionSpec as P

MESH = pl.DeviceIdType.MESH
F32 = jnp.float32
BF16 = jnp.bfloat16

HEADS = 12
CHEADS = 6
HD = 128
SHORT = 4
ROWS = 256
CHIP_ROWS = 2 * ROWS
OWN = HEADS // 2
HALF = 128
BLOCKS = CHIP_ROWS // HALF
REACH = 3
CHUNKS = OWN * BLOCKS
LAG = 3
SLOTS = 4
POOLED = ((0, 3), (3, 2), (5, 1))
SPAN = 2 * REACH * LAG
WIDTH = HEADS * HD
OROWS = HD + 16
LEAD = 24
MROWS = 72
QKV_COLS = 144
OUT_COLS = 96
UNIT = 16
SCALE = math.log2(math.e) / math.sqrt(HD)
NEG = -float(2**100)


def nt(a, b):
    return lax.dot_general(a, b, (((1,), (1,)), ((), ())), preferred_element_type=F32)


def dot(a, b):
    return jnp.dot(a, b, preferred_element_type=F32)


def rounded(x):
    return x.astype(BF16).astype(F32)


def kernel(
    n_ctx, n_sub,
    q_ref, k_ref, v_ref, x_ref, pf_ref, pc_ref, uf_ref, uc_ref, ng_ref, wq_ref, wo_ref,
    out_ref,
    qx, kx, vx, xx, qbuf, oin, oout, vt, fout, fine, mid, summit, pooled, na, wqs, pt, hb,
    kb, vb, osc, att, ah, ls, lb, wof,
    i_sem, x_send, x_recv, q_send, q_recv, o_send, o_recv, f_send, f_recv, e_send, e_recv, w_send, w_recv,
    n_send, n_recv, u_send, u_recv, k_send, k_recv, v_send, v_recv, a_send, a_recv, l_send, l_recv, up_send, up_recv, down_send, down_recv,
):
    ctx = lax.axis_index("ctx")
    sub = lax.axis_index("sub")
    n_chip = n_sub // 2
    n_chips = n_ctx * n_chip
    me = ctx * n_sub + sub
    zc = sub // 2
    core = sub % 2
    other = 1 - core
    chip = ctx * n_chip + zc
    left = (chip + n_chips - 1) % n_chips
    right = (chip + 1) % n_chips
    left_id = (left // n_chip, 2 * (left % n_chip) + core)
    right_id = (right // n_chip, 2 * (right % n_chip) + core)
    right_first = (right // n_chip, 2 * (right % n_chip))
    twin = (ctx, 2 * zc + other)

    barrier = pltpu.get_barrier_semaphore()

    def greet(device):
        pl.semaphore_signal(barrier, inc=1, device_id=device, device_id_type=MESH)

    for near in (left, right):
        for side in range(2):
            greet((near // n_chip, 2 * (near % n_chip) + side))
    for step in range(1, n_sub):
        greet((ctx, (sub + step) % n_sub))
    for step in range(1, n_ctx):
        greet(((ctx + step) % n_ctx, sub))

    def remote(src, dst, send, recv, device):
        return pltpu.make_async_remote_copy(
            src_ref=src, dst_ref=dst, send_sem=send, recv_sem=recv,
            device_id=device, device_id_type=MESH,
        )

    own_rows = pl.ds(pl.multiple_of(core * ROWS, ROWS), ROWS)
    own_lanes = pl.ds(pl.multiple_of(core * OWN * HD, HD), OWN * HD)
    twin_lanes = pl.ds(pl.multiple_of(other * OWN * HD, HD), OWN * HD)
    parts = ((q_ref, qx), (k_ref, kx), (v_ref, vx), (x_ref, xx))

    def inward(n):
        src, dst = parts[n]
        return pltpu.make_async_copy(src.at[:, own_lanes], dst.at[own_rows], i_sem.at[n])

    for n in (2, 0, 1, 3):
        inward(n).start()

    def turned(rows):
        for h in range(OWN):
            vt[h, :, rows] = vx[rows, h * HD : (h + 1) * HD].astype(F32).T.astype(BF16)

    inward(2).wait()
    turned(own_rows)
    inward(0).wait()

    def halves(n):
        src, dst = parts[n]
        return remote(src.at[:, twin_lanes], dst.at[own_rows], x_send.at[n], x_recv.at[n], twin)

    pl.semaphore_wait(barrier, 4 + (n_sub - 1) + (n_ctx - 1))
    for n in (0, 2, 1, 3):
        halves(n).start()

    sibling = (ctx, 2 * zc)

    def weight_copy():
        return remote(wq_ref, wqs, w_send.at[0], w_recv.at[0], sibling)

    @pl.when(core == 1)
    def _():
        weight_copy().start()

    def ring(hop, step, send, recv):
        source = (zc - step * (hop - 1) + n_chip) % n_chip
        src = wo_ref if hop == 1 else wof.at[source]
        target = (zc + step + n_chip) % n_chip
        return remote(src, wof.at[source], send.at[hop], recv.at[hop], (ctx, 2 * target + core))

    def up(hop):
        return ring(hop, 1, up_send, up_recv)

    def down(hop):
        return ring(hop, -1, down_send, down_recv)

    def pass_on(way, hop):
        if hop > 1:
            way(hop - 1).wait_recv()
        way(hop).start()

    n_up, n_down = (n_chip - 1) // 2, n_chip // 2
    wof[zc] = wo_ref[...]
    pass_on(up, 1)

    def lanes(h):
        return pl.ds(pl.multiple_of(h * HD, HD), HD)

    def place(g):
        return g // BLOCKS, (g + BLOCKS - 1) % BLOCKS

    def block_rows(block):
        return pl.ds(pl.multiple_of(block * HALF, HALF), HALF)

    def q_copy(s, g):
        if s == 0:
            h, block = place(g)
            src = qx.at[block_rows(block), lanes(h)]
        else:
            src = qbuf.at[s - 1, g]
        return remote(src, qbuf.at[s, g], q_send.at[s, g % SLOTS], q_recv.at[s, g], left_id)

    def o_copy(s, g):
        return remote(
            oout.at[s - 1, g % SLOTS], oin.at[s - 1, g], o_send.at[s - 1, g % SLOTS],
            o_recv.at[s - 1, g], right_id,
        )

    def f_copy(h, half):
        head = core * OWN + h
        rows = pl.ds(pl.multiple_of(LEAD + half * HALF, 8), HALF)
        return remote(fout.at[h, half], fine.at[head, rows, :], f_send.at[h, half], f_recv.at[h], twin)

    def edge_of(h, device, slot):
        head = core * OWN + h
        return remote(
            fout.at[h, 2 + slot, pl.ds(HALF - 16, 16), :], fine.at[head, pl.ds(8, 16), :],
            e_send.at[h, slot], e_recv.at[h, core], device,
        )

    def forward(s, g):
        if s > 0:
            q_copy(s - 1, g).wait_recv()

        @pl.when(g >= SLOTS)
        def _():
            q_copy(s, g - SLOTS).wait_send()

        q_copy(s, g).start()

    def partial(s, g):
        h, block = place(g)
        keys = kx[:, lanes(h)]
        queries = qx[block_rows(block), lanes(h)] if s == 0 else qbuf[s - 1, g]
        t = nt(keys, queries) * SCALE
        if s == 0 or s == REACH:
            key_row = lax.broadcasted_iota(jnp.int32, t.shape, 0)
            query_row = lax.broadcasted_iota(jnp.int32, t.shape, 1) + block * HALF
            t = jnp.where(key_row <= query_row if s == 0 else key_row > query_row, t, NEG)
        peak = rounded(jnp.max(t, axis=0, keepdims=True))
        p = jnp.exp2(t - peak)
        total = jnp.sum(p, axis=0, keepdims=True)
        summed = dot(vt[h], p.astype(BF16))
        if s > 0:
            peak = jnp.where(chip + s < n_chips, peak, NEG)
        return peak, total, summed

    def settle(s, g, state):
        h, block = place(g)
        peak, total, summed = state
        if s < REACH:
            o_copy(s + 1, g).wait_recv()
            stats = oin[s, g, HD:OROWS, :].astype(F32)
            before = stats[0:1]
            top = jnp.maximum(before, peak)
            a = jnp.exp2(before - top)
            b = jnp.exp2(peak - top)
            summed = oin[s, g, 0:HD, :].astype(F32) * a + summed * b
            total = (stats[1:2] + stats[2:3]) * a + total * b
            peak = top
        if s > 0:
            slot = g % SLOTS

            @pl.when(g >= SLOTS)
            def _():
                o_copy(s, g - SLOTS).wait_send()

            oout[s - 1, slot, 0:HD, :] = summed.astype(BF16)
            high = rounded(total)
            row = lax.broadcasted_iota(jnp.int32, (16, HALF), 0)
            stats = jnp.where(row == 0, peak, jnp.where(row == 1, high, total - high))
            oout[s - 1, slot, HD:OROWS, :] = stats.astype(BF16)
            o_copy(s, g).start()
        else:
            attended = (summed / total).T
            base = xx[block_rows(block), lanes(h)].astype(F32)
            rows = rounded(base + attended)
            head = core * OWN + h
            half = block % 2

            @pl.when(block // 2 == core)
            def _():
                fine[head, pl.ds(pl.multiple_of(LEAD + half * HALF, 8), HALF), :] = rows

            @pl.when(block // 2 != core)
            def _():
                fout[h, half] = rows
                f_copy(h, half).start()

            @pl.when((block == 1) & (core == 1))
            def _():
                fine[head, 8:LEAD, :] = rows[HALF - 16 :, :]

            @pl.when((block == 1) & (core == 0))
            def _():
                fout[h, 2] = rows
                edge_of(h, twin, 0).start()

            @pl.when(block == 3)
            def _():
                fout[h, 3] = rows
                edge_of(h, right_first, 1).start()

    def guarded(i, steps_q, steps_o):
        for s in steps_q:
            g = i - s * LAG

            @pl.when((g >= 0) & (g < CHUNKS))
            def _(s=s, g=g):
                forward(s, g)

        for s in steps_o:
            g = i - (2 * REACH - s) * LAG

            @pl.when((g >= 0) & (g < CHUNKS))
            def _(s=s, g=g):
                if s == REACH:
                    q_copy(s - 1, g).wait_recv()
                settle(s, g, partial(s, g))

    def first(i, carry):
        guarded(i, range(REACH), ())
        return carry

    def ramp_up(i, carry):
        for hop in range(2, n_up + 1):
            @pl.when(i == 4 * hop)
            def _(hop=hop):
                pass_on(up, hop)

        guarded(i, range(REACH), range(REACH, -1, -1))
        return carry

    def steady(i, carry):
        for s in range(REACH):
            g = i - s * LAG

            @pl.when(g < CHUNKS)
            def _(s=s, g=g):
                forward(s, g)

        at = {s: i - (2 * REACH - s) * LAG for s in range(REACH + 1)}
        q_copy(REACH - 1, at[REACH]).wait_recv()
        states = {s: partial(s, at[s]) for s in range(REACH, -1, -1)}
        for s in range(REACH, -1, -1):
            settle(s, at[s], states[s])
        return carry

    def ramp_down(i, carry):
        guarded(i, (), range(REACH - 1, -1, -1))
        return carry

    halves(0).wait_recv()
    lax.fori_loop(0, REACH, first, 0)
    halves(2).wait_recv()
    turned(pl.ds(pl.multiple_of(other * ROWS, ROWS), ROWS))
    inward(1).wait()
    inward(3).wait()
    halves(1).wait_recv()
    halves(3).wait_recv()
    lax.fori_loop(REACH, SPAN, ramp_up, 0)
    lax.fori_loop(SPAN, CHUNKS + REACH * LAG, steady, 0)

    def edge_arrival(h, side):
        head = side * OWN + h
        rim = fine.at[head, pl.ds(8, 16), :]
        pltpu.make_async_copy(rim, rim, e_recv.at[h, side]).wait()

    def pool(h):
        theirs = fine.at[other * OWN + h, pl.ds(LEAD, ROWS), :]
        pltpu.make_async_copy(theirs, theirs, f_recv.at[h]).wait()
        edge_arrival(h, 0)

        @pl.when(core == 0)
        def _():
            edge_arrival(h, 1)

        for side in range(2):
            head = side * OWN + h
            at = slice(head * HD, (head + 1) * HD)
            fine[head, 0:8, :] = jnp.zeros((8, HD), F32)
            fine[head, 8:LEAD, :] = jnp.where(me > 0, fine[head, 8:LEAD, :], 0.0)
            row = jnp.zeros((68, HD), F32)
            for k in range(SHORT):
                row = row + fine[head, pl.ds(LEAD - 19 + k, 68, stride=SHORT), :] * pf_ref[k : k + 1, at]
            mid[head, 0:68, :] = rounded(row)
            row = jnp.zeros((16, HD), F32)
            for k in range(SHORT):
                row = row + mid[head, pl.ds(1 + k, 16, stride=SHORT), :] * pc_ref[k : k + 1, at]
            row = row.astype(BF16)
            summit[:, at] = row.astype(F32)
            pooled[h, :, side * HD : (side + 1) * HD] = row

    def n_copy(batch, step):
        first, count = POOLED[batch]
        target = (zc + step) % n_chip
        span = pl.ds(first, count)
        return remote(
            pooled.at[span], na.at[sub, span], n_send.at[batch, step], n_recv.at[batch, sub], (ctx, 2 * target)
        )

    def n_arrival(batch, source):
        first, count = POOLED[batch]
        span = pl.ds(first, count)
        return remote(
            pooled.at[span], na.at[source, span], n_send.at[batch, 0], n_recv.at[batch, source], sibling
        )

    def share(batch):
        first, count = POOLED[batch]
        for h in range(first, first + count):
            pool(h)
        for step in range(1, n_chip):
            n_copy(batch, step).start()

        @pl.when(core == 1)
        def _():
            n_copy(batch, 0).start()

        @pl.when(core == 0)
        def _():
            na[sub, first : first + count] = pooled[first : first + count]

    share(0)
    pass_on(down, 1)
    lax.fori_loop(CHUNKS + REACH * LAG, CHUNKS + SPAN - 2, ramp_down, 0)
    share(1)
    pass_on(down, 2)
    lax.fori_loop(CHUNKS + SPAN - 2, CHUNKS + SPAN, ramp_down, 0)
    share(2)

    def spread(i):
        unit = 18 * zc + i
        piece = unit // 8
        head = piece % CHEADS
        at = pl.multiple_of((piece // CHEADS) * HD + (unit % 8) * UNIT, UNIT)
        src, dst = pt.at[pl.ds(i * UNIT, UNIT)], hb.at[pl.ds(at, UNIT)]
        return (
            head,
            lambda: remote(src, dst, u_send.at[i], u_recv.at[0], (ctx, 2 * head)),
            lambda: pltpu.make_async_copy(src, dst, u_recv.at[0]),
        )

    def k_copy(source, step):
        return remote(kb.at[source], kb.at[source], k_send.at[step], k_recv.at[source], (source + step, sub))

    def v_copy(source, step):
        return remote(vb.at[source], vb.at[source], v_send.at[step], v_recv.at[source], (source + step, sub))

    def a_copy(step):
        target = (sub + step) % n_sub
        rows = pl.ds(pl.multiple_of((target // 2) * 2 * UNIT, 2 * UNIT), 2 * UNIT)
        return remote(att.at[rows], ah.at[zc], a_send.at[step], a_recv.at[zc], (ctx, target))

    @pl.when(core == 0)
    def _():
        weight_copy().wait_recv()
        for batch in range(len(POOLED)):
            for source in range(n_sub):
                @pl.when(source != sub)
                def _(batch=batch, source=source):
                    n_arrival(batch, source).wait_recv()

        def wide(h):
            return na[:, h].reshape(ROWS, 2 * HD).astype(F32)

        def pair(ref, h):
            head = OWN + h
            return jnp.concatenate([ref[:, h * HD : (h + 1) * HD], ref[:, head * HD : (head + 1) * HD]], axis=1)

        gain = ng_ref[...].reshape(1, WIDTH)
        square = jnp.zeros((ROWS, 1), F32)
        for h in range(OWN):
            square = square + jnp.sum(wide(h) * wide(h), axis=1, keepdims=True)
        scale = lax.rsqrt(square / WIDTH + 1e-05)
        sums = [jnp.zeros((QKV_COLS, ROWS), F32)] * 2
        for h in range(OWN):
            rows = (wide(h) * scale * pair(gain, h)).astype(BF16)
            sums = [total + nt(pair(w, h), rows) for total, w in zip(sums, (wq_ref, wqs))]
        for turn in range(2):
            pt[turn * QKV_COLS : (turn + 1) * QKV_COLS, :] = sums[turn].astype(BF16)
        for i in range(18):
            head, away, here = spread(i)

            @pl.when(head == zc)
            def _(here=here):
                here().start()

            @pl.when(head != zc)
            def _(away=away):
                away().start()

    pass_on(down, 3)

    @pl.when((core == 0) & (zc < CHEADS))
    def _():
        pltpu.make_async_copy(hb, hb, u_recv.at[0]).wait()
        kb[ctx] = hb[HD : 2 * HD].astype(F32).T.astype(BF16)
        vb[ctx] = hb[2 * HD : 3 * HD]
        for step in range(1, n_ctx):
            @pl.when(ctx + step < n_ctx)
            def _(step=step):
                k_copy(ctx, step).start()
                v_copy(ctx, step).start()

    for hop in range(4, n_down + 1):
        pass_on(down, hop)

    @pl.when((core == 0) & (zc < CHEADS))
    def _():
        queries = hb[0:HD].astype(F32).T.astype(BF16)
        t = nt(kb[ctx], queries) * SCALE
        key_row = lax.broadcasted_iota(jnp.int32, t.shape, 0)
        query_row = lax.broadcasted_iota(jnp.int32, t.shape, 1)
        t = jnp.where(key_row <= query_row, t, NEG)
        peak = jnp.max(t, axis=0, keepdims=True)
        p = jnp.exp2(t - peak)
        total = jnp.sum(p, axis=0, keepdims=True)
        osc[...] = dot(vb[ctx], p.astype(BF16))

        def fold(i, carry):
            before, total = carry
            source = ctx - 1 - i
            k_copy(source, 1).wait_recv()
            v_copy(source, 1).wait_recv()
            t = nt(kb[source], queries) * SCALE
            peak = jnp.maximum(before, jnp.max(t, axis=0, keepdims=True))
            p = jnp.exp2(t - peak)
            a = jnp.exp2(before - peak)
            osc[...] = osc[...] * a + dot(vb[source], p.astype(BF16))
            return peak, total * a + jnp.sum(p, axis=0, keepdims=True)

        peak, total = lax.fori_loop(0, ctx, fold, (peak, total))
        att[...] = (osc[...] / total).T.astype(BF16)
        for step in range(1, n_sub):
            a_copy(step).start()
        ah[zc] = att[pl.ds(pl.multiple_of(zc * 2 * UNIT, 2 * UNIT), 2 * UNIT), :]

    up(n_up).wait_recv()
    down(n_down).wait_recv()
    for head in range(CHEADS):
        @pl.when((core == 1) | (head != zc))
        def _(head=head):
            remote(att.at[0 : 2 * UNIT], ah.at[head], a_send.at[0], a_recv.at[head], sibling).wait_recv()
    rows = jnp.concatenate([ah[head] for head in range(CHEADS)], axis=1)
    pad = jnp.zeros((2 * UNIT, HD - OUT_COLS), F32)
    for source in range(n_chip):
        lifted = jnp.concatenate([nt(rows, wof[source]), pad], axis=1).astype(BF16)

        @pl.when(core == 0)
        def _(lifted=lifted, source=source):
            lb[0, source] = lifted[:UNIT]
            ls[source] = lifted[UNIT:]

        @pl.when(core == 1)
        def _(lifted=lifted, source=source):
            lb[1, source] = lifted[UNIT:]
            ls[source] = lifted[:UNIT]

    l_copy = remote(ls, lb.at[core], l_send.at[0], l_recv.at[0], twin)
    l_copy.start()
    remote(ls, lb.at[other], l_send.at[0], l_recv.at[0], twin).wait_recv()
    pieces = []
    for source in range(n_chip):
        for turn in range(2):
            pieces.append(lb[turn, source].astype(F32)[:, :OUT_COLS])
    summit[...] = summit[...] + jnp.concatenate(pieces, axis=1)

    for h in range(HEADS):
        at = slice(h * HD, (h + 1) * HD)
        lift = summit[:, at]
        for k in range(SHORT):
            spots = pl.ds(4 + k, 16, stride=SHORT)
            mid[h, spots, :] = mid[h, spots, :] + uc_ref[k : k + 1, at] * lift
        lift = mid[h, 4:68, :]
        for k in range(SHORT):
            spots = pl.ds(LEAD + k, 64, stride=SHORT)
            fine[h, spots, :] = fine[h, spots, :] + uf_ref[k : k + 1, at] * lift
        out_ref[:, at] = fine[h, LEAD : LEAD + ROWS, :].astype(BF16)

    for n in range(4):
        halves(n).wait_send()
    for s in range(REACH):
        for slot in range(SLOTS):
            q_copy(s, CHUNKS - SLOTS + slot).wait_send()
            o_copy(s + 1, CHUNKS - SLOTS + slot).wait_send()
    for h in range(OWN):
        for half in range(2):
            f_copy(h, half).wait_send()
        edge_of(h, right_first, 1).wait_send()

        @pl.when(core == 0)
        def _(h=h):
            edge_of(h, twin, 0).wait_send()

    @pl.when(core == 1)
    def _():
        weight_copy().wait_send()
        for batch in range(len(POOLED)):
            n_copy(batch, 0).wait_send()

    for batch in range(len(POOLED)):
        for step in range(1, n_chip):
            n_copy(batch, step).wait_send()
    for hop in range(1, n_up + 1):
        up(hop).wait_send()
    for hop in range(1, n_down + 1):
        down(hop).wait_send()
    l_copy.wait_send()

    @pl.when(core == 0)
    def _():
        for i in range(18):
            head, away, here = spread(i)

            @pl.when(head != zc)
            def _(away=away):
                away().wait_send()

    @pl.when((core == 0) & (zc < CHEADS))
    def _():
        for step in range(1, n_ctx):
            @pl.when(ctx + step < n_ctx)
            def _(step=step):
                k_copy(ctx, step).wait_send()
                v_copy(ctx, step).wait_send()
        for step in range(1, n_sub):
            a_copy(step).wait_send()


def solution(mesh):
    n_ctx, n_sub = mesh.shape["ctx"], mesh.shape["sub"]
    n_chip = n_sub // 2
    dma = pltpu.SemaphoreType.DMA

    def shards(stream, q, k, v, pf, pc, uf, uc, ng, wq, wo):
        vmem = pl.BlockSpec(memory_space=pltpu.VMEM)
        return pl.pallas_call(
            functools.partial(kernel, n_ctx, n_sub),
            out_shape=jax.ShapeDtypeStruct((ROWS, WIDTH), BF16),
            in_specs=[pl.BlockSpec(memory_space=pl.ANY)] * 4 + [vmem] * 7,
            out_specs=vmem,
            scratch_shapes=[
                *[pltpu.VMEM((CHIP_ROWS, OWN * HD), BF16)] * 4,
                pltpu.VMEM((REACH, CHUNKS, HALF, HD), BF16),
                pltpu.VMEM((REACH, CHUNKS, OROWS, HALF), BF16),
                pltpu.VMEM((REACH, SLOTS, OROWS, HALF), BF16),
                pltpu.VMEM((OWN, HD, CHIP_ROWS), BF16),
                pltpu.VMEM((OWN, 4, HALF, HD), F32),
                pltpu.VMEM((HEADS, LEAD + ROWS, HD), F32),
                pltpu.VMEM((HEADS, MROWS, HD), F32),
                pltpu.VMEM((16, WIDTH), F32),
                pltpu.VMEM((OWN, 16, 2 * HD), BF16),
                pltpu.VMEM((n_sub, OWN, 16, 2 * HD), BF16),
                pltpu.VMEM((QKV_COLS, WIDTH), BF16),
                pltpu.VMEM((2 * QKV_COLS, ROWS), BF16),
                pltpu.VMEM((3 * HD, ROWS), BF16),
                pltpu.VMEM((n_ctx, ROWS, HD), BF16),
                pltpu.VMEM((n_ctx, HD, ROWS), BF16),
                pltpu.VMEM((HD, ROWS), F32),
                pltpu.VMEM((ROWS, HD), BF16),
                pltpu.VMEM((CHEADS, 2 * UNIT, HD), BF16),
                pltpu.VMEM((n_chip, UNIT, HD), BF16),
                pltpu.VMEM((2, n_chip, UNIT, HD), BF16),
                pltpu.VMEM((n_chip, OUT_COLS, CHEADS * HD), BF16),
                dma((4,)), dma((4,)), dma((4,)),
                dma((REACH, SLOTS)), dma((REACH, CHUNKS)),
                dma((REACH, SLOTS)), dma((REACH, CHUNKS)),
                dma((OWN, 2)), dma((OWN,)),
                dma((OWN, 2)), dma((OWN, 2)),
                dma((1,)), dma((1,)),
                dma((len(POOLED), n_chip)), dma((len(POOLED), n_sub)),
                dma((18,)), dma((1,)),
                dma((n_ctx,)), dma((n_ctx,)),
                dma((n_ctx,)), dma((n_ctx,)),
                dma((n_sub,)), dma((CHEADS,)),
                dma((1,)), dma((1,)),
                dma((n_chip,)), dma((n_chip,)),
                dma((n_chip,)), dma((n_chip,)),
            ],
            compiler_params=pltpu.CompilerParams(
                collective_id=0, has_side_effects=True, vmem_limit_bytes=60 * 2**20
            ),
        )(q, k, v, stream, pf, pc, uf, uc, ng, wq.T, wo.T)

    rows = P(("ctx", "sub"), None)
    return jax.shard_map(
        shards,
        mesh=mesh,
        in_specs=(rows, rows, rows, rows, P(), P(), P(), P(), P(), P(None, "sub"), P(None, "sub")),
        out_specs=rows,
        check_vma=False,
    )
```

```python
import functools
import math

import jax
import jax.numpy as jnp
from jax import lax
from jax.experimental import pallas as pl
from jax.experimental.pallas import tpu as pltpu
from jax.sharding import PartitionSpec as P

MESH = pl.DeviceIdType.MESH
F32 = jnp.float32
BF16 = jnp.bfloat16

HEADS = 12
CHEADS = 6
HD = 128
SHORT = 4
ROWS = 256
CHIP_ROWS = 2 * ROWS
OWN = HEADS // 2
HALF = 128
BLOCKS = CHIP_ROWS // HALF
REACH = 3
CHUNKS = OWN * BLOCKS
LAG = 3
SLOTS = 4
POOLED = ((0, 3), (3, 2), (5, 1))
SPAN = 2 * REACH * LAG
WIDTH = HEADS * HD
LEAD = 24
MROWS = 72
QKV_COLS = 144
OUT_COLS = 96
UNIT = 16
SCALE = math.log2(math.e) / math.sqrt(HD)
NEG = -float(2**100)


def nt(a, b):
    return lax.dot_general(a, b, (((1,), (1,)), ((), ())), preferred_element_type=F32)


def dot(a, b):
    return jnp.dot(a, b, preferred_element_type=F32)


def rounded(x):
    return x.astype(BF16).astype(F32)


def kernel(
    n_ctx, n_sub,
    q_ref, k_ref, v_ref, x_ref, pf_ref, pc_ref, uf_ref, uc_ref, ng_ref, wq_ref, wo_ref,
    out_ref,
    qx, kx, vx, xx, qbuf, oin, oout, sin, sout, vt, fout, fine, mid, summit, pooled, na, wqs, pt, hb,
    kb, vb, osc, att, ah, ls, lb, wof,
    i_sem, x_send, x_recv, q_send, q_recv, o_send, o_recv, s_send, s_recv, f_send, f_recv, e_send, e_recv, w_send, w_recv,
    n_send, n_recv, u_send, u_recv, k_send, k_recv, v_send, v_recv, a_send, a_recv, l_send, l_recv, up_send, up_recv, down_send, down_recv,
):
    ctx = lax.axis_index("ctx")
    sub = lax.axis_index("sub")
    n_chip = n_sub // 2
    n_chips = n_ctx * n_chip
    me = ctx * n_sub + sub
    zc = sub // 2
    core = sub % 2
    other = 1 - core
    chip = ctx * n_chip + zc
    left = (chip + n_chips - 1) % n_chips
    right = (chip + 1) % n_chips
    left_id = (left // n_chip, 2 * (left % n_chip) + core)
    right_id = (right // n_chip, 2 * (right % n_chip) + core)
    right_first = (right // n_chip, 2 * (right % n_chip))
    twin = (ctx, 2 * zc + other)

    barrier = pltpu.get_barrier_semaphore()

    def greet(device):
        pl.semaphore_signal(barrier, inc=1, device_id=device, device_id_type=MESH)

    for step in range(n_ctx - 1, 0, -1):
        greet(((ctx + step) % n_ctx, sub))
    for step in range(1, n_sub):
        greet((ctx, (sub + step) % n_sub))
    for near in (left, right):
        for side in range(2):
            greet((near // n_chip, 2 * (near % n_chip) + side))

    def remote(src, dst, send, recv, device):
        return pltpu.make_async_remote_copy(
            src_ref=src, dst_ref=dst, send_sem=send, recv_sem=recv,
            device_id=device, device_id_type=MESH,
        )

    own_rows = pl.ds(pl.multiple_of(core * ROWS, ROWS), ROWS)
    own_lanes = pl.ds(pl.multiple_of(core * OWN * HD, HD), OWN * HD)
    twin_lanes = pl.ds(pl.multiple_of(other * OWN * HD, HD), OWN * HD)
    parts = ((q_ref, qx), (k_ref, kx), (v_ref, vx), (x_ref, xx))

    def inward(n):
        src, dst = parts[n]
        return pltpu.make_async_copy(src.at[:, own_lanes], dst.at[own_rows], i_sem.at[n])

    for n in (2, 0, 1, 3):
        inward(n).start()

    def turned(rows):
        for h in range(OWN):
            vt[h, :, rows] = vx[rows, h * HD : (h + 1) * HD].astype(F32).T.astype(BF16)

    inward(2).wait()
    turned(own_rows)
    inward(0).wait()

    def halves(n):
        src, dst = parts[n]
        return remote(src.at[:, twin_lanes], dst.at[own_rows], x_send.at[n], x_recv.at[n], twin)

    pl.semaphore_wait(barrier, 4 + (n_sub - 1) + (n_ctx - 1))
    for n in (0, 2, 1, 3):
        halves(n).start()

    sibling = (ctx, 2 * zc)

    def weight_copy():
        return remote(wq_ref, wqs, w_send.at[0], w_recv.at[0], sibling)

    @pl.when(core == 1)
    def _():
        weight_copy().start()

    def ring(hop, step, send, recv):
        source = (zc - step * (hop - 1) + n_chip) % n_chip
        src = wo_ref if hop == 1 else wof.at[source]
        target = (zc + step + n_chip) % n_chip
        return remote(src, wof.at[source], send.at[hop], recv.at[hop], (ctx, 2 * target + core))

    def up(hop):
        return ring(hop, 1, up_send, up_recv)

    def down(hop):
        return ring(hop, -1, down_send, down_recv)

    def pass_on(way, hop):
        if hop > 1:
            way(hop - 1).wait_recv()
        way(hop).start()

    n_up, n_down = (n_chip - 1) // 2, n_chip // 2
    wof[zc] = wo_ref[...]
    pass_on(up, 1)

    def lanes(h):
        return pl.ds(pl.multiple_of(h * HD, HD), HD)

    def place(g):
        turn = g % BLOCKS
        near = turn + 1 - 2 * (turn % 2)
        return g // BLOCKS, near + core * (BLOCKS - 1 - turn - near)

    def block_rows(block):
        return pl.ds(pl.multiple_of(block * HALF, HALF), HALF)

    def q_copy(s, g):
        if s == 0:
            h, block = place(g)
            src = qx.at[block_rows(block), lanes(h)]
        else:
            src = qbuf.at[s - 1, g]
        return remote(src, qbuf.at[s, g], q_send.at[s, g % SLOTS], q_recv.at[s, g], left_id)

    def o_copy(s, g):
        return remote(
            oout.at[s - 1, g % SLOTS], oin.at[s - 1, g], o_send.at[s - 1, g % SLOTS],
            o_recv.at[s - 1, g], right_id,
        )

    def s_copy(s, g):
        return remote(
            sout.at[s - 1, g % SLOTS], sin.at[s - 1, g], s_send.at[s - 1, g % SLOTS],
            s_recv.at[s - 1, g], right_id,
        )

    def f_copy(h, half):
        head = core * OWN + h
        rows = pl.ds(pl.multiple_of(LEAD + half * HALF, 8), HALF)
        return remote(fout.at[h, half], fine.at[head, rows, :], f_send.at[h, half], f_recv.at[h], twin)

    def edge_of(h, device, slot):
        head = core * OWN + h
        return remote(
            fout.at[h, 2 + slot, pl.ds(HALF - 16, 16), :], fine.at[head, pl.ds(8, 16), :],
            e_send.at[h, slot], e_recv.at[h, core], device,
        )

    def forward(s, g):
        if s > 0:
            q_copy(s - 1, g).wait_recv()

        @pl.when(g >= SLOTS)
        def _():
            q_copy(s, g - SLOTS).wait_send()

        q_copy(s, g).start()

    def partial(s, g):
        h, block = place(g)
        keys = kx[:, lanes(h)]
        queries = qx[block_rows(block), lanes(h)] if s == 0 else qbuf[s - 1, g]
        t = nt(keys, queries) * SCALE
        if s == 0 or s == REACH:
            key_row = lax.broadcasted_iota(jnp.int32, t.shape, 0)
            query_row = lax.broadcasted_iota(jnp.int32, t.shape, 1) + block * HALF
            t = jnp.where(key_row <= query_row if s == 0 else key_row > query_row, t, NEG)
        peak = jnp.max(t, axis=0, keepdims=True)
        p = jnp.exp2(t - peak)
        total = jnp.sum(p, axis=0, keepdims=True)
        summed = dot(vt[h], p.astype(BF16))
        if s > 0:
            peak = jnp.where(chip + s < n_chips, peak, NEG)
        return peak, total, summed

    def settle(s, g, state):
        h, block = place(g)
        peak, total, summed = state
        if s < REACH:
            s_copy(s + 1, g).wait_recv()
            before = sin[s, g, 0:1, :]
            top = jnp.maximum(before, peak)
            a = jnp.exp2(before - top)
            b = jnp.exp2(peak - top)
            total = sin[s, g, 1:2, :] * a + total * b
            o_copy(s + 1, g).wait_recv()
            summed = oin[s, g].astype(F32) * a + summed * b
            peak = top
        if s > 0:
            slot = g % SLOTS

            @pl.when(g >= SLOTS)
            def _():
                o_copy(s, g - SLOTS).wait_send()
                s_copy(s, g - SLOTS).wait_send()

            sout[s - 1, slot, 0:1, :] = peak
            sout[s - 1, slot, 1:2, :] = total
            s_copy(s, g).start()
            oout[s - 1, slot] = summed.astype(BF16)
            o_copy(s, g).start()
        else:
            attended = (summed / total).T
            base = xx[block_rows(block), lanes(h)].astype(F32)
            rows = rounded(base + attended)
            head = core * OWN + h
            half = block % 2

            @pl.when(block // 2 == core)
            def _():
                fine[head, pl.ds(pl.multiple_of(LEAD + half * HALF, 8), HALF), :] = rows

            @pl.when(block // 2 != core)
            def _():
                fout[h, half] = rows
                f_copy(h, half).start()

            @pl.when((block == 1) & (core == 1))
            def _():
                fine[head, 8:LEAD, :] = rows[HALF - 16 :, :]

            @pl.when((block == 1) & (core == 0))
            def _():
                fout[h, 2] = rows
                edge_of(h, twin, 0).start()

            @pl.when(block == 3)
            def _():
                fout[h, 3] = rows
                edge_of(h, right_first, 1).start()

    def guarded(i, steps_q, steps_o):
        for s in steps_q:
            g = i - s * LAG

            @pl.when((g >= 0) & (g < CHUNKS))
            def _(s=s, g=g):
                forward(s, g)

        for s in steps_o:
            g = i - (2 * REACH - s) * LAG

            @pl.when((g >= 0) & (g < CHUNKS))
            def _(s=s, g=g):
                if s == REACH:
                    q_copy(s - 1, g).wait_recv()
                settle(s, g, partial(s, g))

    def first(i, carry):
        guarded(jnp.int32(i), range(REACH), ())
        return carry

    def ramp_up(i, carry):
        for hop in range(2, n_up + 1):
            @pl.when(i == 4 * hop)
            def _(hop=hop):
                pass_on(up, hop)

        guarded(i, range(REACH), range(REACH, -1, -1))
        return carry

    def steady(i, carry):
        for s in range(REACH):
            g = i - s * LAG

            @pl.when(g < CHUNKS)
            def _(s=s, g=g):
                forward(s, g)

        at = {s: i - (2 * REACH - s) * LAG for s in range(REACH + 1)}
        q_copy(REACH - 1, at[REACH]).wait_recv()
        states = {s: partial(s, at[s]) for s in range(REACH, -1, -1)}
        for s in range(REACH, -1, -1):
            settle(s, at[s], states[s])
        return carry

    def ramp_down(i, carry):
        guarded(i, (), range(REACH - 1, -1, -1))
        return carry

    first(0, 0)
    first(1, 0)
    halves(0).wait_recv()
    first(2, 0)
    halves(2).wait_recv()
    turned(pl.ds(pl.multiple_of(other * ROWS, ROWS), ROWS))
    inward(1).wait()
    inward(3).wait()
    halves(1).wait_recv()
    halves(3).wait_recv()
    lax.fori_loop(REACH, SPAN, ramp_up, 0)
    lax.fori_loop(SPAN, CHUNKS + REACH * LAG, steady, 0)

    def edge_arrival(h, side):
        head = side * OWN + h
        rim = fine.at[head, pl.ds(8, 16), :]
        pltpu.make_async_copy(rim, rim, e_recv.at[h, side]).wait()

    def pool(h):
        theirs = fine.at[other * OWN + h, pl.ds(LEAD, ROWS), :]
        pltpu.make_async_copy(theirs, theirs, f_recv.at[h]).wait()
        edge_arrival(h, 0)

        @pl.when(core == 0)
        def _():
            edge_arrival(h, 1)

        for side in range(2):
            head = side * OWN + h
            at = slice(head * HD, (head + 1) * HD)
            fine[head, 0:8, :] = jnp.zeros((8, HD), F32)
            fine[head, 8:LEAD, :] = jnp.where(me > 0, fine[head, 8:LEAD, :], 0.0)
            row = jnp.zeros((68, HD), F32)
            for k in range(SHORT):
                row = row + fine[head, pl.ds(LEAD - 19 + k, 68, stride=SHORT), :] * pf_ref[k : k + 1, at]
            mid[head, 0:68, :] = rounded(row)
            row = jnp.zeros((16, HD), F32)
            for k in range(SHORT):
                row = row + mid[head, pl.ds(1 + k, 16, stride=SHORT), :] * pc_ref[k : k + 1, at]
            row = row.astype(BF16)
            summit[:, at] = row.astype(F32)
            pooled[h, :, side * HD : (side + 1) * HD] = row

    def n_copy(batch, step):
        first, count = POOLED[batch]
        target = (zc + step) % n_chip
        span = pl.ds(first, count)
        return remote(
            pooled.at[span], na.at[sub, span], n_send.at[batch, step], n_recv.at[batch, sub], (ctx, 2 * target)
        )

    def n_arrival(batch, source):
        first, count = POOLED[batch]
        span = pl.ds(first, count)
        return remote(
            pooled.at[span], na.at[source, span], n_send.at[batch, 0], n_recv.at[batch, source], sibling
        )

    def share(batch):
        first, count = POOLED[batch]
        for h in range(first, first + count):
            pool(h)
        for step in range(1, n_chip):
            n_copy(batch, step).start()

        @pl.when(core == 1)
        def _():
            n_copy(batch, 0).start()

        @pl.when(core == 0)
        def _():
            na[sub, first : first + count] = pooled[first : first + count]

    share(0)
    pass_on(down, 1)
    lax.fori_loop(CHUNKS + REACH * LAG, CHUNKS + SPAN - 2, ramp_down, 0)
    share(1)
    pass_on(down, 2)
    lax.fori_loop(CHUNKS + SPAN - 2, CHUNKS + SPAN, ramp_down, 0)
    share(2)

    def spread(i):
        unit = 18 * zc + i
        piece = unit // 8
        head = piece % CHEADS
        at = pl.multiple_of((piece // CHEADS) * HD + (unit % 8) * UNIT, UNIT)
        src, dst = pt.at[pl.ds(i * UNIT, UNIT)], hb.at[pl.ds(at, UNIT)]
        return (
            head,
            lambda: remote(src, dst, u_send.at[i], u_recv.at[0], (ctx, 2 * head)),
            lambda: pltpu.make_async_copy(src, dst, u_recv.at[0]),
        )

    def k_copy(source, step):
        return remote(kb.at[source], kb.at[source], k_send.at[step], k_recv.at[source], (source + step, sub))

    def v_copy(source, step):
        return remote(vb.at[source], vb.at[source], v_send.at[step], v_recv.at[source], (source + step, sub))

    def a_copy(step):
        target = (sub + step) % n_sub
        rows = pl.ds(pl.multiple_of((target // 2) * 2 * UNIT, 2 * UNIT), 2 * UNIT)
        return remote(att.at[rows], ah.at[zc], a_send.at[step], a_recv.at[zc], (ctx, target))

    @pl.when(core == 0)
    def _():
        weight_copy().wait_recv()
        def wide(h):
            return na[:, h].reshape(ROWS, 2 * HD).astype(F32)

        def pair(ref, h):
            head = OWN + h
            return jnp.concatenate([ref[:, h * HD : (h + 1) * HD], ref[:, head * HD : (head + 1) * HD]], axis=1)

        gain = ng_ref[...].reshape(1, WIDTH)
        square = jnp.zeros((ROWS, 1), F32)
        for batch, (start, count) in enumerate(POOLED):
            for source in range(n_sub):
                @pl.when(source != sub)
                def _(batch=batch, source=source):
                    n_arrival(batch, source).wait_recv()
            for h in range(start, start + count):
                square = square + jnp.sum(wide(h) * wide(h), axis=1, keepdims=True)
        scale = lax.rsqrt(square / WIDTH + 1e-05)
        sums = [jnp.zeros((QKV_COLS, ROWS), F32)] * 2
        for h in range(OWN):
            rows = (wide(h) * scale * pair(gain, h)).astype(BF16)
            sums = [total + nt(pair(w, h), rows) for total, w in zip(sums, (wq_ref, wqs))]
        for turn in range(2):
            pt[turn * QKV_COLS : (turn + 1) * QKV_COLS, :] = sums[turn].astype(BF16)
        for i in range(18):
            head, away, here = spread(i)

            @pl.when(head == zc)
            def _(here=here):
                here().start()

            @pl.when(head != zc)
            def _(away=away):
                away().start()

    pass_on(down, 3)

    @pl.when((core == 0) & (zc < CHEADS))
    def _():
        pltpu.make_async_copy(hb, hb, u_recv.at[0]).wait()
        kb[ctx] = hb[HD : 2 * HD].astype(F32).T.astype(BF16)
        vb[ctx] = hb[2 * HD : 3 * HD]
        for step in range(1, n_ctx):
            @pl.when(ctx + step < n_ctx)
            def _(step=step):
                k_copy(ctx, step).start()
                v_copy(ctx, step).start()

    for hop in range(4, n_down + 1):
        pass_on(down, hop)

    for h in range(HEADS):
        at = slice(h * HD, (h + 1) * HD)
        row = summit[:, at]
        for k in range(SHORT):
            spots = pl.ds(4 + k, 16, stride=SHORT)
            mid[h, spots, :] = mid[h, spots, :] + uc_ref[k : k + 1, at] * row
        row = mid[h, 4:68, :]
        for k in range(SHORT):
            spots = pl.ds(LEAD + k, 64, stride=SHORT)
            fine[h, spots, :] = fine[h, spots, :] + uf_ref[k : k + 1, at] * row

    @pl.when((core == 0) & (zc < CHEADS))
    def _():
        queries = hb[0:HD].astype(F32).T.astype(BF16)
        t = nt(kb[ctx], queries) * SCALE
        key_row = lax.broadcasted_iota(jnp.int32, t.shape, 0)
        query_row = lax.broadcasted_iota(jnp.int32, t.shape, 1)
        t = jnp.where(key_row <= query_row, t, NEG)
        peak = jnp.max(t, axis=0, keepdims=True)
        p = jnp.exp2(t - peak)
        total = jnp.sum(p, axis=0, keepdims=True)
        osc[...] = dot(vb[ctx], p.astype(BF16))

        def fold(i, carry):
            before, total = carry
            source = ctx - 1 - i
            k_copy(source, 1).wait_recv()
            v_copy(source, 1).wait_recv()
            t = nt(kb[source], queries) * SCALE
            peak = jnp.maximum(before, jnp.max(t, axis=0, keepdims=True))
            p = jnp.exp2(t - peak)
            a = jnp.exp2(before - peak)
            osc[...] = osc[...] * a + dot(vb[source], p.astype(BF16))
            return peak, total * a + jnp.sum(p, axis=0, keepdims=True)

        peak, total = lax.fori_loop(0, ctx, fold, (peak, total))
        att[...] = (osc[...] / total).T.astype(BF16)
        for step in range(1, n_sub):
            a_copy(step).start()
        ah[zc] = att[pl.ds(pl.multiple_of(zc * 2 * UNIT, 2 * UNIT), 2 * UNIT), :]

    up(n_up).wait_recv()
    down(n_down).wait_recv()
    for head in range(CHEADS):
        @pl.when((core == 1) | (head != zc))
        def _(head=head):
            remote(att.at[0 : 2 * UNIT], ah.at[head], a_send.at[0], a_recv.at[head], sibling).wait_recv()
    rows = jnp.concatenate([ah[head] for head in range(CHEADS)], axis=1)
    both = nt(rows, wof[...].reshape(n_chip * OUT_COLS, CHEADS * HD)).astype(BF16)

    @pl.when(core == 0)
    def _():
        lb[0] = both[:UNIT]
        ls[...] = both[UNIT:]

    @pl.when(core == 1)
    def _():
        lb[1] = both[UNIT:]
        ls[...] = both[:UNIT]

    l_copy = remote(ls, lb.at[core], l_send.at[0], l_recv.at[0], twin)
    l_copy.start()
    remote(ls, lb.at[other], l_send.at[0], l_recv.at[0], twin).wait_recv()
    sides = [lb[side].astype(F32) for side in range(2)]
    pieces = []
    for source in range(n_chip):
        for side in range(2):
            pieces.append(sides[side][:, source * OUT_COLS : (source + 1) * OUT_COLS])
    lifted = jnp.concatenate(pieces, axis=1)

    for h in range(HEADS):
        at = slice(h * HD, (h + 1) * HD)
        up_rows = [uc_ref[j : j + 1, at] * uf_ref[:, at] for j in range(SHORT)]
        factor = jnp.concatenate(up_rows, axis=0)
        for r in range(UNIT):
            rows = slice(r * 16, (r + 1) * 16)
            base = fine[h, LEAD + r * 16 : LEAD + (r + 1) * 16, :]
            out_ref[rows, at] = (base + factor * lifted[r : r + 1, at]).astype(BF16)

    for n in range(4):
        halves(n).wait_send()
    for s in range(REACH):
        for slot in range(SLOTS):
            q_copy(s, CHUNKS - SLOTS + slot).wait_send()
            o_copy(s + 1, CHUNKS - SLOTS + slot).wait_send()
            s_copy(s + 1, CHUNKS - SLOTS + slot).wait_send()
    for h in range(OWN):
        for half in range(2):
            f_copy(h, half).wait_send()
        edge_of(h, right_first, 1).wait_send()

        @pl.when(core == 0)
        def _(h=h):
            edge_of(h, twin, 0).wait_send()

    @pl.when(core == 1)
    def _():
        weight_copy().wait_send()
        for batch in range(len(POOLED)):
            n_copy(batch, 0).wait_send()

    for batch in range(len(POOLED)):
        for step in range(1, n_chip):
            n_copy(batch, step).wait_send()
    for hop in range(1, n_up + 1):
        up(hop).wait_send()
    for hop in range(1, n_down + 1):
        down(hop).wait_send()
    l_copy.wait_send()

    @pl.when(core == 0)
    def _():
        for i in range(18):
            head, away, here = spread(i)

            @pl.when(head != zc)
            def _(away=away):
                away().wait_send()

    @pl.when((core == 0) & (zc < CHEADS))
    def _():
        for step in range(1, n_ctx):
            @pl.when(ctx + step < n_ctx)
            def _(step=step):
                k_copy(ctx, step).wait_send()
                v_copy(ctx, step).wait_send()
        for step in range(1, n_sub):
            a_copy(step).wait_send()


def solution(mesh):
    n_ctx, n_sub = mesh.shape["ctx"], mesh.shape["sub"]
    n_chip = n_sub // 2
    dma = pltpu.SemaphoreType.DMA

    def shards(stream, q, k, v, pf, pc, uf, uc, ng, wq, wo):
        vmem = pl.BlockSpec(memory_space=pltpu.VMEM)
        return pl.pallas_call(
            functools.partial(kernel, n_ctx, n_sub),
            out_shape=jax.ShapeDtypeStruct((ROWS, WIDTH), BF16),
            in_specs=[pl.BlockSpec(memory_space=pl.ANY)] * 4 + [vmem] * 7,
            out_specs=vmem,
            scratch_shapes=[
                *[pltpu.VMEM((CHIP_ROWS, OWN * HD), BF16)] * 4,
                pltpu.VMEM((REACH, CHUNKS, HALF, HD), BF16),
                pltpu.VMEM((REACH, CHUNKS, HD, HALF), BF16),
                pltpu.VMEM((REACH, SLOTS, HD, HALF), BF16),
                pltpu.VMEM((REACH, CHUNKS, 2, HALF), F32),
                pltpu.VMEM((REACH, SLOTS, 2, HALF), F32),
                pltpu.VMEM((OWN, HD, CHIP_ROWS), BF16),
                pltpu.VMEM((OWN, 4, HALF, HD), F32),
                pltpu.VMEM((HEADS, LEAD + ROWS, HD), F32),
                pltpu.VMEM((HEADS, MROWS, HD), F32),
                pltpu.VMEM((16, WIDTH), F32),
                pltpu.VMEM((OWN, 16, 2 * HD), BF16),
                pltpu.VMEM((n_sub, OWN, 16, 2 * HD), BF16),
                pltpu.VMEM((QKV_COLS, WIDTH), BF16),
                pltpu.VMEM((2 * QKV_COLS, ROWS), BF16),
                pltpu.VMEM((3 * HD, ROWS), BF16),
                pltpu.VMEM((n_ctx, ROWS, HD), BF16),
                pltpu.VMEM((n_ctx, HD, ROWS), BF16),
                pltpu.VMEM((HD, ROWS), F32),
                pltpu.VMEM((ROWS, HD), BF16),
                pltpu.VMEM((CHEADS, 2 * UNIT, HD), BF16),
                pltpu.VMEM((UNIT, n_chip * OUT_COLS), BF16),
                pltpu.VMEM((2, UNIT, n_chip * OUT_COLS), BF16),
                pltpu.VMEM((n_chip, OUT_COLS, CHEADS * HD), BF16),
                dma((4,)), dma((4,)), dma((4,)),
                dma((REACH, SLOTS)), dma((REACH, CHUNKS)),
                dma((REACH, SLOTS)), dma((REACH, CHUNKS)),
                dma((REACH, SLOTS)), dma((REACH, CHUNKS)),
                dma((OWN, 2)), dma((OWN,)),
                dma((OWN, 2)), dma((OWN, 2)),
                dma((1,)), dma((1,)),
                dma((len(POOLED), n_chip)), dma((len(POOLED), n_sub)),
                dma((18,)), dma((1,)),
                dma((n_ctx,)), dma((n_ctx,)),
                dma((n_ctx,)), dma((n_ctx,)),
                dma((n_sub,)), dma((CHEADS,)),
                dma((1,)), dma((1,)),
                dma((n_chip,)), dma((n_chip,)),
                dma((n_chip,)), dma((n_chip,)),
            ],
            compiler_params=pltpu.CompilerParams(
                collective_id=0, has_side_effects=True, vmem_limit_bytes=60 * 2**20
            ),
        )(q, k, v, stream, pf, pc, uf, uc, ng, wq.T, wo.T)

    rows = P(("ctx", "sub"), None)
    return jax.shard_map(
        shards,
        mesh=mesh,
        in_specs=(rows, rows, rows, rows, P(), P(), P(), P(), P(), P(None, "sub"), P(None, "sub")),
        out_specs=rows,
        check_vma=False,
    )
```

```python
import functools
import math

import jax
import jax.numpy as jnp
from jax import lax
from jax.experimental import pallas as pl
from jax.experimental.pallas import tpu as pltpu
from jax.sharding import PartitionSpec as P

MESH = pl.DeviceIdType.MESH
F32 = jnp.float32
BF16 = jnp.bfloat16

HEADS = 12
CHEADS = 6
HD = 128
SHORT = 4
ROWS = 256
CHIP_ROWS = 2 * ROWS
OWN = HEADS // 2
HALF = 128
BLOCKS = CHIP_ROWS // HALF
REACH = 3
CHUNKS = OWN * BLOCKS
Q_AT = (0, 2, 5, 8)
O_AT = (17, 14, 11, 8)
SLOTS = 4
POOLED = ((0, 3), (3, 2), (5, 1))
SPAN = O_AT[0]
WIDTH = HEADS * HD
LEAD = 24
MROWS = 72
QKV_COLS = 144
OUT_COLS = 96
UNIT = 16
SCALE = math.log2(math.e) / math.sqrt(HD)
NEG = -float(2**100)


def nt(a, b):
    return lax.dot_general(a, b, (((1,), (1,)), ((), ())), preferred_element_type=F32)


def dot(a, b):
    return jnp.dot(a, b, preferred_element_type=F32)


def rounded(x):
    return x.astype(BF16).astype(F32)


def kernel(
    n_ctx, n_sub,
    q_ref, k_ref, v_ref, x_ref, pf_ref, pc_ref, uf_ref, uc_ref, ng_ref, wq_ref, wo_ref,
    out_ref,
    qx, kx, vx, xx, qbuf, oin, oout, sin, sout, vt, fout, fine, mid, summit, pooled, na, wqs, pt, hb,
    kv, osc, att, ah, ls, lb, wof,
    i_sem, x_send, x_recv, q_send, q_recv, o_send, o_recv, s_send, s_recv, f_send, f_recv, e_send, e_recv, w_send, w_recv,
    n_send, n_recv, u_send, u_recv, k_send, k_recv, a_send, a_recv, l_send, l_recv, up_send, up_recv, down_send, down_recv,
):
    ctx = lax.axis_index("ctx")
    sub = lax.axis_index("sub")
    n_chip = n_sub // 2
    n_chips = n_ctx * n_chip
    me = ctx * n_sub + sub
    zc = sub // 2
    core = sub % 2
    other = 1 - core
    chip = ctx * n_chip + zc
    left = (chip + n_chips - 1) % n_chips
    right = (chip + 1) % n_chips
    left_id = (left // n_chip, 2 * (left % n_chip) + core)
    right_id = (right // n_chip, 2 * (right % n_chip) + core)
    right_first = (right // n_chip, 2 * (right % n_chip))
    twin = (ctx, 2 * zc + other)

    barrier = pltpu.get_barrier_semaphore()

    def greet(device):
        pl.semaphore_signal(barrier, inc=1, device_id=device, device_id_type=MESH)

    for step in range(n_ctx - 1, 0, -1):
        greet(((ctx + step) % n_ctx, sub))
    for step in range(1, n_sub):
        greet((ctx, (sub + step) % n_sub))
    for near in (left, right):
        for side in range(2):
            greet((near // n_chip, 2 * (near % n_chip) + side))

    def remote(src, dst, send, recv, device):
        return pltpu.make_async_remote_copy(
            src_ref=src, dst_ref=dst, send_sem=send, recv_sem=recv,
            device_id=device, device_id_type=MESH,
        )

    own_rows = pl.ds(pl.multiple_of(core * ROWS, ROWS), ROWS)
    own_lanes = pl.ds(pl.multiple_of(core * OWN * HD, HD), OWN * HD)
    twin_lanes = pl.ds(pl.multiple_of(other * OWN * HD, HD), OWN * HD)
    parts = ((q_ref, qx), (k_ref, kx), (v_ref, vx), (x_ref, xx))

    def inward(n):
        src, dst = parts[n]
        return pltpu.make_async_copy(src.at[:, own_lanes], dst.at[own_rows], i_sem.at[n])

    for n in (2, 0, 1, 3):
        inward(n).start()

    def turned(rows):
        for h in range(OWN):
            vt[h, :, rows] = vx[rows, h * HD : (h + 1) * HD].astype(F32).T.astype(BF16)

    inward(2).wait()
    turned(own_rows)
    inward(0).wait()

    def halves(n):
        src, dst = parts[n]
        return remote(src.at[:, twin_lanes], dst.at[own_rows], x_send.at[n], x_recv.at[n], twin)

    pl.semaphore_wait(barrier, 4 + (n_sub - 1) + (n_ctx - 1))
    for n in (0, 2, 1, 3):
        halves(n).start()

    sibling = (ctx, 2 * zc)

    def weight_copy():
        return remote(wq_ref, wqs, w_send.at[0], w_recv.at[0], sibling)

    @pl.when(core == 1)
    def _():
        weight_copy().start()

    def ring(hop, step, send, recv):
        source = (zc - step * (hop - 1) + n_chip) % n_chip
        src = wo_ref if hop == 1 else wof.at[source]
        target = (zc + step + n_chip) % n_chip
        return remote(src, wof.at[source], send.at[hop], recv.at[hop], (ctx, 2 * target + core))

    def up(hop):
        return ring(hop, 1, up_send, up_recv)

    def down(hop):
        return ring(hop, -1, down_send, down_recv)

    def pass_on(way, hop):
        if hop > 1:
            way(hop - 1).wait_recv()
        way(hop).start()

    n_up, n_down = (n_chip - 1) // 2, n_chip // 2
    wof[zc] = wo_ref[...]
    pass_on(up, 1)

    def lanes(h):
        return pl.ds(pl.multiple_of(h * HD, HD), HD)

    def place(g):
        turn = g % BLOCKS
        near = turn + 1 - 2 * (turn % 2)
        return g // BLOCKS, near + core * (BLOCKS - 1 - turn - near)

    def block_rows(block):
        return pl.ds(pl.multiple_of(block * HALF, HALF), HALF)

    def q_copy(s, g):
        if s == 0:
            h, block = place(g)
            src = qx.at[block_rows(block), lanes(h)]
        else:
            src = qbuf.at[s - 1, g]
        return remote(src, qbuf.at[s, g], q_send.at[s, g % SLOTS], q_recv.at[s, g], left_id)

    def o_copy(s, g):
        return remote(
            oout.at[s - 1, g % SLOTS], oin.at[s - 1, g], o_send.at[s - 1, g % SLOTS],
            o_recv.at[s - 1, g], right_id,
        )

    def s_copy(s, g):
        return remote(
            sout.at[s - 1, g % SLOTS], sin.at[s - 1, g], s_send.at[s - 1, g % SLOTS],
            s_recv.at[s - 1, g], right_id,
        )

    def f_copy(h, half):
        head = core * OWN + h
        rows = pl.ds(pl.multiple_of(LEAD + half * HALF, 8), HALF)
        return remote(fout.at[h, half], fine.at[head, rows, :], f_send.at[h, half], f_recv.at[h], twin)

    def edge_of(h, device, slot):
        head = core * OWN + h
        return remote(
            fout.at[h, 2 + slot, pl.ds(HALF - 16, 16), :], fine.at[head, pl.ds(8, 16), :],
            e_send.at[h, slot], e_recv.at[h, core], device,
        )

    def forward(s, g):
        if s > 0:
            q_copy(s - 1, g).wait_recv()

        @pl.when(g >= SLOTS)
        def _():
            q_copy(s, g - SLOTS).wait_send()

        q_copy(s, g).start()

    def partial(s, g):
        h, block = place(g)
        keys = kx[:, lanes(h)]
        queries = qx[block_rows(block), lanes(h)] if s == 0 else qbuf[s - 1, g]
        t = nt(keys, queries) * SCALE
        if s == 0 or s == REACH:
            key_row = lax.broadcasted_iota(jnp.int32, t.shape, 0)
            query_row = lax.broadcasted_iota(jnp.int32, t.shape, 1) + block * HALF
            t = jnp.where(key_row <= query_row if s == 0 else key_row > query_row, t, NEG)
        peak = jnp.max(t, axis=0, keepdims=True)
        p = jnp.exp2(t - peak)
        total = jnp.sum(p, axis=0, keepdims=True)
        summed = dot(vt[h], p.astype(BF16))
        if s > 0:
            peak = jnp.where(chip + s < n_chips, peak, NEG)
        return peak, total, summed

    def settle(s, g, state):
        h, block = place(g)
        peak, total, summed = state
        if s < REACH:
            s_copy(s + 1, g).wait_recv()
            before = sin[s, g, 0:1, :]
            top = jnp.maximum(before, peak)
            a = jnp.exp2(before - top)
            b = jnp.exp2(peak - top)
            total = sin[s, g, 1:2, :] * a + total * b
            o_copy(s + 1, g).wait_recv()
            summed = oin[s, g].astype(F32) * a + summed * b
            peak = top
        if s > 0:
            slot = g % SLOTS

            @pl.when(g >= SLOTS)
            def _():
                o_copy(s, g - SLOTS).wait_send()
                s_copy(s, g - SLOTS).wait_send()

            sout[s - 1, slot, 0:1, :] = peak
            sout[s - 1, slot, 1:2, :] = total
            s_copy(s, g).start()
            oout[s - 1, slot] = summed.astype(BF16)
            o_copy(s, g).start()
        else:
            attended = (summed / total).T
            base = xx[block_rows(block), lanes(h)].astype(F32)
            rows = rounded(base + attended)
            head = core * OWN + h
            half = block % 2

            @pl.when(block // 2 == core)
            def _():
                fine[head, pl.ds(pl.multiple_of(LEAD + half * HALF, 8), HALF), :] = rows

            @pl.when(block // 2 != core)
            def _():
                fout[h, half] = rows
                f_copy(h, half).start()

            @pl.when((block == 1) & (core == 1))
            def _():
                fine[head, 8:LEAD, :] = rows[HALF - 16 :, :]

            @pl.when((block == 1) & (core == 0))
            def _():
                fout[h, 2] = rows
                edge_of(h, twin, 0).start()

            @pl.when(block == 3)
            def _():
                fout[h, 3] = rows
                edge_of(h, right_first, 1).start()

    def guarded(i, steps_q, steps_o):
        for s in steps_q:
            g = i - Q_AT[s]

            @pl.when((g >= 0) & (g < CHUNKS))
            def _(s=s, g=g):
                forward(s, g)

        for s in steps_o:
            g = i - O_AT[s]

            @pl.when((g >= 0) & (g < CHUNKS))
            def _(s=s, g=g):
                if s == REACH:
                    q_copy(s - 1, g).wait_recv()
                settle(s, g, partial(s, g))

    def first(i, carry):
        guarded(jnp.int32(i), range(REACH), ())
        return carry

    def ramp_up(i, carry):
        for hop in range(2, n_up + 1):
            @pl.when(i == 4 * hop)
            def _(hop=hop):
                pass_on(up, hop)

        guarded(i, range(REACH), range(REACH, -1, -1))
        return carry

    def steady(i, carry):
        for s in range(REACH):
            g = i - Q_AT[s]

            @pl.when(g < CHUNKS)
            def _(s=s, g=g):
                forward(s, g)

        at = {s: i - O_AT[s] for s in range(REACH + 1)}
        q_copy(REACH - 1, at[REACH]).wait_recv()
        states = {s: partial(s, at[s]) for s in range(REACH, -1, -1)}
        for s in range(REACH, -1, -1):
            settle(s, at[s], states[s])
        return carry

    def ramp_down(i, carry):
        guarded(i, (), range(REACH - 1, -1, -1))
        return carry

    first(0, 0)
    first(1, 0)
    halves(0).wait_recv()
    first(2, 0)
    halves(2).wait_recv()
    turned(pl.ds(pl.multiple_of(other * ROWS, ROWS), ROWS))
    inward(1).wait()
    inward(3).wait()
    halves(1).wait_recv()
    halves(3).wait_recv()
    lax.fori_loop(REACH, SPAN, ramp_up, 0)
    lax.fori_loop(SPAN, CHUNKS + O_AT[REACH], steady, 0)

    def edge_arrival(h, side):
        head = side * OWN + h
        rim = fine.at[head, pl.ds(8, 16), :]
        pltpu.make_async_copy(rim, rim, e_recv.at[h, side]).wait()

    def pool(h):
        theirs = fine.at[other * OWN + h, pl.ds(LEAD, ROWS), :]
        pltpu.make_async_copy(theirs, theirs, f_recv.at[h]).wait()
        edge_arrival(h, 0)

        @pl.when(core == 0)
        def _():
            edge_arrival(h, 1)

        for side in range(2):
            head = side * OWN + h
            at = slice(head * HD, (head + 1) * HD)
            fine[head, 0:8, :] = jnp.zeros((8, HD), F32)
            fine[head, 8:LEAD, :] = jnp.where(me > 0, fine[head, 8:LEAD, :], 0.0)
            row = jnp.zeros((68, HD), F32)
            for k in range(SHORT):
                row = row + fine[head, pl.ds(LEAD - 19 + k, 68, stride=SHORT), :] * pf_ref[k : k + 1, at]
            mid[head, 0:68, :] = rounded(row)
            row = jnp.zeros((16, HD), F32)
            for k in range(SHORT):
                row = row + mid[head, pl.ds(1 + k, 16, stride=SHORT), :] * pc_ref[k : k + 1, at]
            row = row.astype(BF16)
            summit[:, at] = row.astype(F32)
            pooled[h, :, side * HD : (side + 1) * HD] = row

    def n_copy(batch, step):
        first, count = POOLED[batch]
        target = (zc + step) % n_chip
        span = pl.ds(first, count)
        return remote(
            pooled.at[span], na.at[sub, span], n_send.at[batch, step], n_recv.at[batch, sub], (ctx, 2 * target)
        )

    def n_arrival(batch, source):
        first, count = POOLED[batch]
        span = pl.ds(first, count)
        return remote(
            pooled.at[span], na.at[source, span], n_send.at[batch, 0], n_recv.at[batch, source], sibling
        )

    def share(batch):
        first, count = POOLED[batch]
        for h in range(first, first + count):
            pool(h)
        for step in sorted(range(1, n_chip), key=lambda step: abs(step - n_chip // 2)):
            n_copy(batch, step).start()

        @pl.when(core == 1)
        def _():
            n_copy(batch, 0).start()

        @pl.when(core == 0)
        def _():
            na[sub, first : first + count] = pooled[first : first + count]

    share(0)
    pass_on(down, 1)
    lax.fori_loop(CHUNKS + O_AT[REACH], CHUNKS + SPAN - 2, ramp_down, 0)
    share(1)
    pass_on(down, 2)
    lax.fori_loop(CHUNKS + SPAN - 2, CHUNKS + SPAN, ramp_down, 0)
    share(2)

    def spread(i):
        unit = 18 * zc + i
        piece = unit // 8
        head = piece % CHEADS
        at = pl.multiple_of((piece // CHEADS) * HD + (unit % 8) * UNIT, UNIT)
        kind = (piece // CHEADS + 1) // 2
        src, dst = pt.at[pl.ds(i * UNIT, UNIT)], hb.at[pl.ds(at, UNIT)]
        return (
            head,
            lambda: remote(src, dst, u_send.at[i], u_recv.at[kind], (ctx, 2 * head)),
            lambda: pltpu.make_async_copy(src, dst, u_recv.at[kind]),
        )

    def k_copy(source, step):
        return remote(kv.at[source], kv.at[source], k_send.at[step], k_recv.at[source], (source + step, sub))

    def a_copy(step):
        target = (sub + step) % n_sub
        rows = pl.ds(pl.multiple_of((target // 2) * 2 * UNIT, 2 * UNIT), 2 * UNIT)
        return remote(att.at[rows], ah.at[zc], a_send.at[step], a_recv.at[zc], (ctx, target))

    @pl.when(core == 0)
    def _():
        weight_copy().wait_recv()
        def wide(h):
            return na[:, h].reshape(ROWS, 2 * HD).astype(F32)

        def pair(ref, h):
            head = OWN + h
            return jnp.concatenate([ref[:, h * HD : (h + 1) * HD], ref[:, head * HD : (head + 1) * HD]], axis=1)

        gain = ng_ref[...].reshape(1, WIDTH)
        square = jnp.zeros((ROWS, 1), F32)
        for batch, (start, count) in enumerate(POOLED):
            for source in range(n_sub):
                @pl.when(source != sub)
                def _(batch=batch, source=source):
                    n_arrival(batch, source).wait_recv()
            for h in range(start, start + count):
                square = square + jnp.sum(wide(h) * wide(h), axis=1, keepdims=True)
        scale = lax.rsqrt(square / WIDTH + 1e-05)
        sums = [jnp.zeros((QKV_COLS, ROWS), F32)] * 2
        for h in range(OWN):
            rows = (wide(h) * scale * pair(gain, h)).astype(BF16)
            sums = [total + nt(pair(w, h), rows) for total, w in zip(sums, (wq_ref, wqs))]
        for turn in range(2):
            pt[turn * QKV_COLS : (turn + 1) * QKV_COLS, :] = sums[turn].astype(BF16)
        for i in range(18):
            head, away, here = spread(i)

            @pl.when(head == zc)
            def _(here=here):
                here().start()

            @pl.when(head != zc)
            def _(away=away):
                away().start()

    pass_on(down, 3)

    @pl.when((core == 0) & (zc < CHEADS))
    def _():
        pair = hb.at[pl.ds(HD, 2 * HD)]
        pltpu.make_async_copy(pair, pair, u_recv.at[1]).wait()
        kv[ctx] = hb[HD : 3 * HD]
        for step in range(1, n_ctx):
            @pl.when(ctx + step < n_ctx)
            def _(step=step):
                k_copy(ctx, step).start()

    for hop in range(4, n_down + 1):
        pass_on(down, hop)

    for h in range(HEADS):
        at = slice(h * HD, (h + 1) * HD)
        row = summit[:, at]
        for k in range(SHORT):
            spots = pl.ds(4 + k, 16, stride=SHORT)
            mid[h, spots, :] = mid[h, spots, :] + uc_ref[k : k + 1, at] * row
        row = mid[h, 4:68, :]
        for k in range(SHORT):
            spots = pl.ds(LEAD + k, 64, stride=SHORT)
            fine[h, spots, :] = fine[h, spots, :] + uf_ref[k : k + 1, at] * row

    @pl.when((core == 0) & (zc < CHEADS))
    def _():
        first = hb.at[pl.ds(0, HD)]
        pltpu.make_async_copy(first, first, u_recv.at[0]).wait()
        queries = hb[0:HD].astype(F32).T.astype(BF16)

        def scored(source):
            return nt(kv[source, 0:HD].astype(F32).T.astype(BF16), queries) * SCALE

        t = scored(ctx)
        key_row = lax.broadcasted_iota(jnp.int32, t.shape, 0)
        query_row = lax.broadcasted_iota(jnp.int32, t.shape, 1)
        t = jnp.where(key_row <= query_row, t, NEG)
        peak = jnp.max(t, axis=0, keepdims=True)
        p = jnp.exp2(t - peak)
        total = jnp.sum(p, axis=0, keepdims=True)
        osc[...] = dot(kv[ctx, HD : 2 * HD], p.astype(BF16))

        def fold(i, carry):
            before, total = carry
            source = ctx - 1 - i
            k_copy(source, 1).wait_recv()
            t = scored(source)
            peak = jnp.maximum(before, jnp.max(t, axis=0, keepdims=True))
            p = jnp.exp2(t - peak)
            a = jnp.exp2(before - peak)
            osc[...] = osc[...] * a + dot(kv[source, HD : 2 * HD], p.astype(BF16))
            return peak, total * a + jnp.sum(p, axis=0, keepdims=True)

        peak, total = lax.fori_loop(0, ctx, fold, (peak, total))
        att[...] = (osc[...] / total).T.astype(BF16)
        for step in sorted(range(1, n_sub), key=lambda step: abs(step - n_sub // 2)):
            a_copy(step).start()
        ah[zc] = att[pl.ds(pl.multiple_of(zc * 2 * UNIT, 2 * UNIT), 2 * UNIT), :]

    up(n_up).wait_recv()
    down(n_down).wait_recv()
    for head in range(CHEADS):
        @pl.when((core == 1) | (head != zc))
        def _(head=head):
            remote(att.at[0 : 2 * UNIT], ah.at[head], a_send.at[0], a_recv.at[head], sibling).wait_recv()
    rows = jnp.concatenate([ah[head] for head in range(CHEADS)], axis=1)
    both = nt(rows, wof[...].reshape(n_chip * OUT_COLS, CHEADS * HD)).astype(BF16)

    @pl.when(core == 0)
    def _():
        lb[0] = both[:UNIT]
        ls[...] = both[UNIT:]

    @pl.when(core == 1)
    def _():
        lb[1] = both[UNIT:]
        ls[...] = both[:UNIT]

    l_copy = remote(ls, lb.at[core], l_send.at[0], l_recv.at[0], twin)
    l_copy.start()
    remote(ls, lb.at[other], l_send.at[0], l_recv.at[0], twin).wait_recv()
    sides = [lb[side].astype(F32) for side in range(2)]
    pieces = []
    for source in range(n_chip):
        for side in range(2):
            pieces.append(sides[side][:, source * OUT_COLS : (source + 1) * OUT_COLS])
    lifted = jnp.concatenate(pieces, axis=1)

    for h in range(HEADS):
        at = slice(h * HD, (h + 1) * HD)
        up_rows = [uc_ref[j : j + 1, at] * uf_ref[:, at] for j in range(SHORT)]
        factor = jnp.concatenate(up_rows, axis=0)
        for r in range(UNIT):
            rows = slice(r * 16, (r + 1) * 16)
            base = fine[h, LEAD + r * 16 : LEAD + (r + 1) * 16, :]
            out_ref[rows, at] = (base + factor * lifted[r : r + 1, at]).astype(BF16)

    for n in range(4):
        halves(n).wait_send()
    for s in range(REACH):
        for slot in range(SLOTS):
            q_copy(s, CHUNKS - SLOTS + slot).wait_send()
            o_copy(s + 1, CHUNKS - SLOTS + slot).wait_send()
            s_copy(s + 1, CHUNKS - SLOTS + slot).wait_send()
    for h in range(OWN):
        for half in range(2):
            f_copy(h, half).wait_send()
        edge_of(h, right_first, 1).wait_send()

        @pl.when(core == 0)
        def _(h=h):
            edge_of(h, twin, 0).wait_send()

    @pl.when(core == 1)
    def _():
        weight_copy().wait_send()
        for batch in range(len(POOLED)):
            n_copy(batch, 0).wait_send()

    for batch in range(len(POOLED)):
        for step in range(1, n_chip):
            n_copy(batch, step).wait_send()
    for hop in range(1, n_up + 1):
        up(hop).wait_send()
    for hop in range(1, n_down + 1):
        down(hop).wait_send()
    l_copy.wait_send()

    @pl.when(core == 0)
    def _():
        for i in range(18):
            head, away, here = spread(i)

            @pl.when(head != zc)
            def _(away=away):
                away().wait_send()

    @pl.when((core == 0) & (zc < CHEADS))
    def _():
        for step in range(1, n_ctx):
            @pl.when(ctx + step < n_ctx)
            def _(step=step):
                k_copy(ctx, step).wait_send()
        for step in range(1, n_sub):
            a_copy(step).wait_send()


def solution(mesh):
    n_ctx, n_sub = mesh.shape["ctx"], mesh.shape["sub"]
    n_chip = n_sub // 2
    dma = pltpu.SemaphoreType.DMA

    def shards(stream, q, k, v, pf, pc, uf, uc, ng, wq, wo):
        vmem = pl.BlockSpec(memory_space=pltpu.VMEM)
        return pl.pallas_call(
            functools.partial(kernel, n_ctx, n_sub),
            out_shape=jax.ShapeDtypeStruct((ROWS, WIDTH), BF16),
            in_specs=[pl.BlockSpec(memory_space=pl.ANY)] * 4 + [vmem] * 7,
            out_specs=vmem,
            scratch_shapes=[
                *[pltpu.VMEM((CHIP_ROWS, OWN * HD), BF16)] * 4,
                pltpu.VMEM((REACH, CHUNKS, HALF, HD), BF16),
                pltpu.VMEM((REACH, CHUNKS, HD, HALF), BF16),
                pltpu.VMEM((REACH, SLOTS, HD, HALF), BF16),
                pltpu.VMEM((REACH, CHUNKS, 2, HALF), F32),
                pltpu.VMEM((REACH, SLOTS, 2, HALF), F32),
                pltpu.VMEM((OWN, HD, CHIP_ROWS), BF16),
                pltpu.VMEM((OWN, 4, HALF, HD), F32),
                pltpu.VMEM((HEADS, LEAD + ROWS, HD), F32),
                pltpu.VMEM((HEADS, MROWS, HD), F32),
                pltpu.VMEM((16, WIDTH), F32),
                pltpu.VMEM((OWN, 16, 2 * HD), BF16),
                pltpu.VMEM((n_sub, OWN, 16, 2 * HD), BF16),
                pltpu.VMEM((QKV_COLS, WIDTH), BF16),
                pltpu.VMEM((2 * QKV_COLS, ROWS), BF16),
                pltpu.VMEM((3 * HD, ROWS), BF16),
                pltpu.VMEM((n_ctx, 2 * HD, ROWS), BF16),
                pltpu.VMEM((HD, ROWS), F32),
                pltpu.VMEM((ROWS, HD), BF16),
                pltpu.VMEM((CHEADS, 2 * UNIT, HD), BF16),
                pltpu.VMEM((UNIT, n_chip * OUT_COLS), BF16),
                pltpu.VMEM((2, UNIT, n_chip * OUT_COLS), BF16),
                pltpu.VMEM((n_chip, OUT_COLS, CHEADS * HD), BF16),
                dma((4,)), dma((4,)), dma((4,)),
                dma((REACH, SLOTS)), dma((REACH, CHUNKS)),
                dma((REACH, SLOTS)), dma((REACH, CHUNKS)),
                dma((REACH, SLOTS)), dma((REACH, CHUNKS)),
                dma((OWN, 2)), dma((OWN,)),
                dma((OWN, 2)), dma((OWN, 2)),
                dma((1,)), dma((1,)),
                dma((len(POOLED), n_chip)), dma((len(POOLED), n_sub)),
                dma((18,)), dma((2,)),
                dma((n_ctx,)), dma((n_ctx,)),
                dma((n_sub,)), dma((CHEADS,)),
                dma((1,)), dma((1,)),
                dma((n_chip,)), dma((n_chip,)),
                dma((n_chip,)), dma((n_chip,)),
            ],
            compiler_params=pltpu.CompilerParams(
                collective_id=0, has_side_effects=True, vmem_limit_bytes=60 * 2**20
            ),
        )(q, k, v, stream, pf, pc, uf, uc, ng, wq.T, wo.T)

    rows = P(("ctx", "sub"), None)
    return jax.shard_map(
        shards,
        mesh=mesh,
        in_specs=(rows, rows, rows, rows, P(), P(), P(), P(), P(), P(None, "sub"), P(None, "sub")),
        out_specs=rows,
        check_vma=False,
    )
```

```python
import functools
import math

import jax
import jax.numpy as jnp
from jax import lax
from jax.experimental import pallas as pl
from jax.experimental.pallas import tpu as pltpu
from jax.sharding import PartitionSpec as P

MESH = pl.DeviceIdType.MESH
F32 = jnp.float32
BF16 = jnp.bfloat16

HEADS = 12
CHEADS = 6
HD = 128
SHORT = 4
ROWS = 256
CHIP_ROWS = 2 * ROWS
OWN = HEADS // 2
HALF = 128
BLOCKS = CHIP_ROWS // HALF
REACH = 3
CHUNKS = OWN * BLOCKS
Q_AT = (0, 2, 5, 8)
O_AT = (17, 14, 11, 8)
SLOTS = 4
POOLED = ((0, 3), (3, 2), (5, 1))
SPAN = O_AT[0]
WIDTH = HEADS * HD
LEAD = 24
MROWS = 72
QKV_COLS = 144
OUT_COLS = 96
UNIT = 16
SCALE = math.log2(math.e) / math.sqrt(HD)
NEG = -float(2**100)


def nt(a, b):
    return lax.dot_general(a, b, (((1,), (1,)), ((), ())), preferred_element_type=F32)


def dot(a, b):
    return jnp.dot(a, b, preferred_element_type=F32)


def rounded(x):
    return x.astype(BF16).astype(F32)


def kernel(
    n_ctx, n_sub,
    q_ref, k_ref, v_ref, x_ref, pf_ref, pc_ref, uf_ref, uc_ref, ng_ref, wq_ref, wo_ref,
    out_ref,
    qx, kx, vx, xx, qbuf, oin, oout, sin, sout, vt, fout, fine, mid, summit, pooled, na, wqs, pt, hb,
    kv, osc, att, ah, ls, lb, wof,
    i_sem, x_send, x_recv, q_send, q_recv, o_send, o_recv, s_send, s_recv, f_send, f_recv, e_send, e_recv, w_send, w_recv,
    n_send, n_recv, u_send, u_recv, k_send, k_recv, a_send, a_recv, l_send, l_recv, up_send, up_recv, down_send, down_recv,
):
    ctx = lax.axis_index("ctx")
    sub = lax.axis_index("sub")
    n_chip = n_sub // 2
    n_chips = n_ctx * n_chip
    me = ctx * n_sub + sub
    zc = sub // 2
    core = sub % 2
    other = 1 - core
    chip = ctx * n_chip + zc
    left = (chip + n_chips - 1) % n_chips
    right = (chip + 1) % n_chips
    left_id = (left // n_chip, 2 * (left % n_chip) + core)
    right_id = (right // n_chip, 2 * (right % n_chip) + core)
    right_first = (right // n_chip, 2 * (right % n_chip))
    twin = (ctx, 2 * zc + other)

    barrier = pltpu.get_barrier_semaphore()

    def greet(device):
        pl.semaphore_signal(barrier, inc=1, device_id=device, device_id_type=MESH)

    for step in range(n_ctx - 1, 0, -1):
        greet(((ctx + step) % n_ctx, sub))
    for step in range(1, n_sub):
        greet((ctx, (sub + step) % n_sub))
    for near in (left, right):
        for side in range(2):
            greet((near // n_chip, 2 * (near % n_chip) + side))

    def remote(src, dst, send, recv, device):
        return pltpu.make_async_remote_copy(
            src_ref=src, dst_ref=dst, send_sem=send, recv_sem=recv,
            device_id=device, device_id_type=MESH,
        )

    own_rows = pl.ds(pl.multiple_of(core * ROWS, ROWS), ROWS)
    own_lanes = pl.ds(pl.multiple_of(core * OWN * HD, HD), OWN * HD)
    twin_lanes = pl.ds(pl.multiple_of(other * OWN * HD, HD), OWN * HD)
    parts = ((q_ref, qx), (k_ref, kx), (v_ref, vx), (x_ref, xx))

    def inward(n):
        src, dst = parts[n]
        return pltpu.make_async_copy(src.at[:, own_lanes], dst.at[own_rows], i_sem.at[n])

    for n in (2, 0, 1, 3):
        inward(n).start()

    def turned(rows):
        for h in range(OWN):
            vt[h, :, rows] = vx[rows, h * HD : (h + 1) * HD].astype(F32).T.astype(BF16)

    inward(2).wait()
    turned(own_rows)
    inward(0).wait()

    def halves(n):
        src, dst = parts[n]
        return remote(src.at[:, twin_lanes], dst.at[own_rows], x_send.at[n], x_recv.at[n], twin)

    pl.semaphore_wait(barrier, 4 + (n_sub - 1) + (n_ctx - 1))
    for n in (0, 2, 1, 3):
        halves(n).start()

    sibling = (ctx, 2 * zc)

    def weight_copy():
        return remote(wq_ref, wqs, w_send.at[0], w_recv.at[0], sibling)

    @pl.when(core == 1)
    def _():
        weight_copy().start()

    def ring(hop, step, send, recv):
        source = (zc - step * (hop - 1) + n_chip) % n_chip
        src = wo_ref if hop == 1 else wof.at[source]
        target = (zc + step + n_chip) % n_chip
        return remote(src, wof.at[source], send.at[hop], recv.at[hop], (ctx, 2 * target + core))

    def up(hop):
        return ring(hop, 1, up_send, up_recv)

    def down(hop):
        return ring(hop, -1, down_send, down_recv)

    def pass_on(way, hop):
        if hop > 1:
            way(hop - 1).wait_recv()
        way(hop).start()

    n_up, n_down = (n_chip - 1) // 2, n_chip // 2
    wof[zc] = wo_ref[...]
    pass_on(up, 1)

    def lanes(h):
        return pl.ds(pl.multiple_of(h * HD, HD), HD)

    def place(g):
        turn = g % BLOCKS
        near = turn + 1 - 2 * (turn % 2)
        return g // BLOCKS, near + core * (BLOCKS - 1 - turn - near)

    def block_rows(block):
        return pl.ds(pl.multiple_of(block * HALF, HALF), HALF)

    def q_copy(s, g):
        if s == 0:
            h, block = place(g)
            src = qx.at[block_rows(block), lanes(h)]
        else:
            src = qbuf.at[s - 1, g]
        return remote(src, qbuf.at[s, g], q_send.at[s, g % SLOTS], q_recv.at[s, g], left_id)

    def o_copy(s, g):
        return remote(
            oout.at[s - 1, g % SLOTS], oin.at[s - 1, g], o_send.at[s - 1, g % SLOTS],
            o_recv.at[s - 1, g], right_id,
        )

    def s_copy(s, g):
        return remote(
            sout.at[s - 1, g % SLOTS], sin.at[s - 1, g], s_send.at[s - 1, g % SLOTS],
            s_recv.at[s - 1, g], right_id,
        )

    def f_copy(h, half):
        head = core * OWN + h
        rows = pl.ds(pl.multiple_of(LEAD + half * HALF, 8), HALF)
        return remote(fout.at[h, half], fine.at[head, rows, :], f_send.at[h, half], f_recv.at[h], twin)

    def edge_of(h, device, slot):
        head = core * OWN + h
        return remote(
            fout.at[h, 2 + slot, pl.ds(HALF - 16, 16), :], fine.at[head, pl.ds(8, 16), :],
            e_send.at[h, slot], e_recv.at[h, core], device,
        )

    def forward(s, g):
        if s > 0:
            q_copy(s - 1, g).wait_recv()

        @pl.when(g >= SLOTS)
        def _():
            q_copy(s, g - SLOTS).wait_send()

        q_copy(s, g).start()

    def partial(s, g):
        h, block = place(g)
        keys = kx[:, lanes(h)]
        queries = qx[block_rows(block), lanes(h)] if s == 0 else qbuf[s - 1, g]
        t = nt(keys, queries) * SCALE
        if s == 0 or s == REACH:
            key_row = lax.broadcasted_iota(jnp.int32, t.shape, 0)
            query_row = lax.broadcasted_iota(jnp.int32, t.shape, 1) + block * HALF
            t = jnp.where(key_row <= query_row if s == 0 else key_row > query_row, t, NEG)
        peak = jnp.max(t, axis=0, keepdims=True)
        p = jnp.exp2(t - peak)
        total = jnp.sum(p, axis=0, keepdims=True)
        summed = dot(vt[h], p.astype(BF16))
        if s > 0:
            peak = jnp.where(chip + s < n_chips, peak, NEG)
        return peak, total, summed

    def settle(s, g, state):
        h, block = place(g)
        peak, total, summed = state
        if s < REACH:
            s_copy(s + 1, g).wait_recv()
            before = sin[s, g, 0:1, :]
            top = jnp.maximum(before, peak)
            a = jnp.exp2(before - top)
            b = jnp.exp2(peak - top)
            total = sin[s, g, 1:2, :] * a + total * b
            o_copy(s + 1, g).wait_recv()
            summed = oin[s, g].astype(F32) * a + summed * b
            peak = top
        if s > 0:
            slot = g % SLOTS

            @pl.when(g >= SLOTS)
            def _():
                o_copy(s, g - SLOTS).wait_send()
                s_copy(s, g - SLOTS).wait_send()

            sout[s - 1, slot, 0:1, :] = peak
            sout[s - 1, slot, 1:2, :] = total
            s_copy(s, g).start()
            oout[s - 1, slot] = summed.astype(BF16)
            o_copy(s, g).start()
        else:
            attended = (summed / total).T
            base = xx[block_rows(block), lanes(h)].astype(F32)
            rows = rounded(base + attended)
            head = core * OWN + h
            half = block % 2

            @pl.when(block // 2 == core)
            def _():
                fine[head, pl.ds(pl.multiple_of(LEAD + half * HALF, 8), HALF), :] = rows

            @pl.when(block // 2 != core)
            def _():
                fout[h, half] = rows
                f_copy(h, half).start()

            @pl.when((block == 1) & (core == 1))
            def _():
                fine[head, 8:LEAD, :] = rows[HALF - 16 :, :]

            @pl.when((block == 1) & (core == 0))
            def _():
                fout[h, 2] = rows
                edge_of(h, twin, 0).start()

            @pl.when(block == 3)
            def _():
                fout[h, 3] = rows
                edge_of(h, right_first, 1).start()

    def guarded(i, steps_q, steps_o):
        for s in steps_q:
            g = i - Q_AT[s]

            @pl.when((g >= 0) & (g < CHUNKS))
            def _(s=s, g=g):
                forward(s, g)

        for s in steps_o:
            g = i - O_AT[s]

            @pl.when((g >= 0) & (g < CHUNKS))
            def _(s=s, g=g):
                if s == REACH:
                    q_copy(s - 1, g).wait_recv()
                settle(s, g, partial(s, g))

    def first(i, carry):
        guarded(jnp.int32(i), range(REACH), ())
        return carry

    def ramp_up(i, carry):
        for hop in range(2, n_up + 1):
            @pl.when(i == 4 * hop)
            def _(hop=hop):
                pass_on(up, hop)

        guarded(i, range(REACH), range(REACH, -1, -1))
        return carry

    def steady(i, carry):
        for s in range(REACH):
            g = i - Q_AT[s]

            @pl.when(g < CHUNKS)
            def _(s=s, g=g):
                forward(s, g)

        at = {s: i - O_AT[s] for s in range(REACH + 1)}
        q_copy(REACH - 1, at[REACH]).wait_recv()
        states = {s: partial(s, at[s]) for s in range(REACH, -1, -1)}
        for s in range(REACH, -1, -1):
            settle(s, at[s], states[s])
        return carry

    def ramp_down(i, carry):
        guarded(i, (), range(REACH - 1, -1, -1))
        return carry

    first(0, 0)
    first(1, 0)
    halves(0).wait_recv()
    first(2, 0)
    halves(2).wait_recv()
    turned(pl.ds(pl.multiple_of(other * ROWS, ROWS), ROWS))
    inward(1).wait()
    inward(3).wait()
    halves(1).wait_recv()
    halves(3).wait_recv()
    lax.fori_loop(REACH, SPAN, ramp_up, 0)
    lax.fori_loop(SPAN, CHUNKS + O_AT[REACH], steady, 0)

    def edge_arrival(h, side):
        head = side * OWN + h
        rim = fine.at[head, pl.ds(8, 16), :]
        pltpu.make_async_copy(rim, rim, e_recv.at[h, side]).wait()

    def pool(h):
        theirs = fine.at[other * OWN + h, pl.ds(LEAD, ROWS), :]
        pltpu.make_async_copy(theirs, theirs, f_recv.at[h]).wait()
        edge_arrival(h, 0)

        @pl.when(core == 0)
        def _():
            edge_arrival(h, 1)

        for side in range(2):
            head = side * OWN + h
            at = slice(head * HD, (head + 1) * HD)
            fine[head, 0:8, :] = jnp.zeros((8, HD), F32)
            fine[head, 8:LEAD, :] = jnp.where(me > 0, fine[head, 8:LEAD, :], 0.0)
            row = jnp.zeros((68, HD), F32)
            for k in range(SHORT):
                row = row + fine[head, pl.ds(LEAD - 19 + k, 68, stride=SHORT), :] * pf_ref[k : k + 1, at]
            mid[head, 0:68, :] = rounded(row)
            row = jnp.zeros((16, HD), F32)
            for k in range(SHORT):
                row = row + mid[head, pl.ds(1 + k, 16, stride=SHORT), :] * pc_ref[k : k + 1, at]
            row = row.astype(BF16)
            summit[:, at] = row.astype(F32)
            pooled[h, :, side * HD : (side + 1) * HD] = row

    def n_copy(batch, step):
        first, count = POOLED[batch]
        target = (zc + step) % n_chip
        span = pl.ds(first, count)
        return remote(
            pooled.at[span], na.at[sub, span], n_send.at[batch, step], n_recv.at[batch, sub], (ctx, 2 * target)
        )

    def n_arrival(batch, source):
        first, count = POOLED[batch]
        span = pl.ds(first, count)
        return remote(
            pooled.at[span], na.at[source, span], n_send.at[batch, 0], n_recv.at[batch, source], sibling
        )

    def share(batch):
        first, count = POOLED[batch]
        for h in range(first, first + count):
            pool(h)
        for step in sorted(range(1, n_chip), key=lambda step: abs(step - n_chip // 2)):
            n_copy(batch, step).start()

        @pl.when(core == 1)
        def _():
            n_copy(batch, 0).start()

        @pl.when(core == 0)
        def _():
            na[sub, first : first + count] = pooled[first : first + count]

    share(0)
    pass_on(down, 1)
    lax.fori_loop(CHUNKS + O_AT[REACH], CHUNKS + SPAN - 2, ramp_down, 0)
    share(1)
    pass_on(down, 2)
    lax.fori_loop(CHUNKS + SPAN - 2, CHUNKS + SPAN, ramp_down, 0)
    share(2)

    def spread(i):
        unit = 18 * zc + i
        piece = unit // 8
        head = piece % CHEADS
        at = pl.multiple_of((piece // CHEADS) * HD + (unit % 8) * UNIT, UNIT)
        kind = (piece // CHEADS + 1) // 2
        src, dst = pt.at[pl.ds(i * UNIT, UNIT)], hb.at[pl.ds(at, UNIT)]
        return (
            head,
            lambda: remote(src, dst, u_send.at[i], u_recv.at[kind], (ctx, 2 * head)),
            lambda: pltpu.make_async_copy(src, dst, u_recv.at[kind]),
        )

    def k_copy(source, step):
        return remote(kv.at[source], kv.at[source], k_send.at[step], k_recv.at[source], (source + step, sub))

    def a_copy(step):
        target = (sub + step) % n_sub
        rows = pl.ds(pl.multiple_of((target // 2) * 2 * UNIT, 2 * UNIT), 2 * UNIT)
        return remote(att.at[rows], ah.at[zc], a_send.at[step], a_recv.at[zc], (ctx, target))

    @pl.when(core == 0)
    def _():
        weight_copy().wait_recv()
        def wide(h):
            return na[:, h].reshape(ROWS, 2 * HD).astype(F32)

        def pair(ref, h):
            head = OWN + h
            return jnp.concatenate([ref[:, h * HD : (h + 1) * HD], ref[:, head * HD : (head + 1) * HD]], axis=1)

        gain = ng_ref[...].reshape(1, WIDTH)
        square = jnp.zeros((ROWS, 1), F32)
        for batch, (start, count) in enumerate(POOLED):
            for source in range(n_sub):
                @pl.when(source != sub)
                def _(batch=batch, source=source):
                    n_arrival(batch, source).wait_recv()
            for h in range(start, start + count):
                square = square + jnp.sum(wide(h) * wide(h), axis=1, keepdims=True)
        scale = lax.rsqrt(square / WIDTH + 1e-05)
        sums = [jnp.zeros((QKV_COLS, ROWS), F32)] * 2
        for h in range(OWN):
            rows = (wide(h) * scale * pair(gain, h)).astype(BF16)
            sums = [total + nt(pair(w, h), rows) for total, w in zip(sums, (wq_ref, wqs))]
        for turn in range(2):
            pt[turn * QKV_COLS : (turn + 1) * QKV_COLS, :] = sums[turn].astype(BF16)
        for i in range(18):
            head, away, here = spread(i)

            @pl.when(head == zc)
            def _(here=here):
                here().start()

            @pl.when(head != zc)
            def _(away=away):
                away().start()

    pass_on(down, 3)

    @pl.when((core == 0) & (zc < CHEADS))
    def _():
        pair = hb.at[pl.ds(HD, 2 * HD)]
        pltpu.make_async_copy(pair, pair, u_recv.at[1]).wait()
        kv[ctx] = hb[HD : 3 * HD]
        for step in range(1, n_ctx):
            @pl.when(ctx + step < n_ctx)
            def _(step=step):
                k_copy(ctx, step).start()

    for hop in range(4, n_down + 1):
        pass_on(down, hop)

    for h in range(HEADS):
        at = slice(h * HD, (h + 1) * HD)
        row = summit[:, at]
        for k in range(SHORT):
            spots = pl.ds(4 + k, 16, stride=SHORT)
            mid[h, spots, :] = mid[h, spots, :] + uc_ref[k : k + 1, at] * row
        row = mid[h, 4:68, :]
        for k in range(SHORT):
            spots = pl.ds(LEAD + k, 64, stride=SHORT)
            fine[h, spots, :] = fine[h, spots, :] + uf_ref[k : k + 1, at] * row

    @pl.when((core == 0) & (zc < CHEADS))
    def _():
        first = hb.at[pl.ds(0, HD)]
        pltpu.make_async_copy(first, first, u_recv.at[0]).wait()
        queries = hb[0:HD].astype(F32).T.astype(BF16)

        def scored(source):
            return nt(kv[source, 0:HD].astype(F32).T.astype(BF16), queries) * SCALE

        t = scored(ctx)
        key_row = lax.broadcasted_iota(jnp.int32, t.shape, 0)
        query_row = lax.broadcasted_iota(jnp.int32, t.shape, 1)
        t = jnp.where(key_row <= query_row, t, NEG)
        peak = jnp.max(t, axis=0, keepdims=True)
        p = jnp.exp2(t - peak)
        total = jnp.sum(p, axis=0, keepdims=True)
        osc[...] = dot(kv[ctx, HD : 2 * HD], p.astype(BF16))

        def fold(i, carry):
            before, total = carry
            source = ctx - 1 - i
            k_copy(source, 1).wait_recv()
            t = scored(source)
            peak = jnp.maximum(before, jnp.max(t, axis=0, keepdims=True))
            p = jnp.exp2(t - peak)
            a = jnp.exp2(before - peak)
            osc[...] = osc[...] * a + dot(kv[source, HD : 2 * HD], p.astype(BF16))
            return peak, total * a + jnp.sum(p, axis=0, keepdims=True)

        peak, total = lax.fori_loop(0, ctx, fold, (peak, total))
        att[...] = (osc[...] / total).T.astype(BF16)
        for step in sorted(range(1, n_sub), key=lambda step: abs(step - n_sub // 2)):
            a_copy(step).start()
        ah[zc] = att[pl.ds(pl.multiple_of(zc * 2 * UNIT, 2 * UNIT), 2 * UNIT), :]

    up(n_up).wait_recv()
    down(n_down).wait_recv()
    for head in range(CHEADS):
        @pl.when((core == 1) | (head != zc))
        def _(head=head):
            remote(att.at[0 : 2 * UNIT], ah.at[head], a_send.at[0], a_recv.at[head], sibling).wait_recv()
    rows = jnp.concatenate([ah[head] for head in range(CHEADS)], axis=1)
    both = nt(rows, wof[...].reshape(n_chip * OUT_COLS, CHEADS * HD)).astype(BF16)

    @pl.when(core == 0)
    def _():
        lb[0] = both[:UNIT]
        ls[...] = both[UNIT:]

    @pl.when(core == 1)
    def _():
        lb[1] = both[UNIT:]
        ls[...] = both[:UNIT]

    l_copy = remote(ls, lb.at[core], l_send.at[0], l_recv.at[0], twin)
    l_copy.start()
    remote(ls, lb.at[other], l_send.at[0], l_recv.at[0], twin).wait_recv()
    sides = [lb[side].astype(F32) for side in range(2)]
    pieces = []
    for source in range(n_chip):
        for side in range(2):
            pieces.append(sides[side][:, source * OUT_COLS : (source + 1) * OUT_COLS])
    lifted = jnp.concatenate(pieces, axis=1)

    for h in range(HEADS):
        at = slice(h * HD, (h + 1) * HD)
        up_rows = [uc_ref[j : j + 1, at] * uf_ref[:, at] for j in range(SHORT)]
        factor = jnp.concatenate(up_rows, axis=0)
        for r in range(UNIT):
            rows = slice(r * 16, (r + 1) * 16)
            base = fine[h, LEAD + r * 16 : LEAD + (r + 1) * 16, :]
            out_ref[rows, at] = (base + factor * lifted[r : r + 1, at]).astype(BF16)

    for n in range(4):
        halves(n).wait_send()
    for s in range(REACH):
        for slot in range(SLOTS):
            q_copy(s, CHUNKS - SLOTS + slot).wait_send()
            o_copy(s + 1, CHUNKS - SLOTS + slot).wait_send()
            s_copy(s + 1, CHUNKS - SLOTS + slot).wait_send()
    for h in range(OWN):
        for half in range(2):
            f_copy(h, half).wait_send()
        edge_of(h, right_first, 1).wait_send()

        @pl.when(core == 0)
        def _(h=h):
            edge_of(h, twin, 0).wait_send()

    @pl.when(core == 1)
    def _():
        weight_copy().wait_send()
        for batch in range(len(POOLED)):
            n_copy(batch, 0).wait_send()

    for batch in range(len(POOLED)):
        for step in range(1, n_chip):
            n_copy(batch, step).wait_send()
    for hop in range(1, n_up + 1):
        up(hop).wait_send()
    for hop in range(1, n_down + 1):
        down(hop).wait_send()
    l_copy.wait_send()

    @pl.when(core == 0)
    def _():
        for i in range(18):
            head, away, here = spread(i)

            @pl.when(head != zc)
            def _(away=away):
                away().wait_send()

    @pl.when((core == 0) & (zc < CHEADS))
    def _():
        for step in range(1, n_ctx):
            @pl.when(ctx + step < n_ctx)
            def _(step=step):
                k_copy(ctx, step).wait_send()
        for step in range(1, n_sub):
            a_copy(step).wait_send()


def solution(mesh):
    n_ctx, n_sub = mesh.shape["ctx"], mesh.shape["sub"]
    n_chip = n_sub // 2
    dma = pltpu.SemaphoreType.DMA

    def shards(stream, q, k, v, pf, pc, uf, uc, ng, wq, wo):
        vmem = pl.BlockSpec(memory_space=pltpu.VMEM)
        return pl.pallas_call(
            functools.partial(kernel, n_ctx, n_sub),
            out_shape=jax.ShapeDtypeStruct((ROWS, WIDTH), BF16),
            in_specs=[pl.BlockSpec(memory_space=pl.ANY)] * 4 + [vmem] * 7,
            out_specs=vmem,
            scratch_shapes=[
                *[pltpu.VMEM((CHIP_ROWS, OWN * HD), BF16)] * 4,
                pltpu.VMEM((REACH, CHUNKS, HALF, HD), BF16),
                pltpu.VMEM((REACH, CHUNKS, HD, HALF), BF16),
                pltpu.VMEM((REACH, SLOTS, HD, HALF), BF16),
                pltpu.VMEM((REACH, CHUNKS, 2, HALF), F32),
                pltpu.VMEM((REACH, SLOTS, 2, HALF), F32),
                pltpu.VMEM((OWN, HD, CHIP_ROWS), BF16),
                pltpu.VMEM((OWN, 4, HALF, HD), F32),
                pltpu.VMEM((HEADS, LEAD + ROWS + 24, HD), F32),
                pltpu.VMEM((HEADS, MROWS, HD), F32),
                pltpu.VMEM((16, WIDTH), F32),
                pltpu.VMEM((OWN, 16, 2 * HD), BF16),
                pltpu.VMEM((n_sub, OWN, 16, 2 * HD), BF16),
                pltpu.VMEM((QKV_COLS, WIDTH), BF16),
                pltpu.VMEM((2 * QKV_COLS, ROWS), BF16),
                pltpu.VMEM((3 * HD, ROWS), BF16),
                pltpu.VMEM((n_ctx, 2 * HD, ROWS), BF16),
                pltpu.VMEM((HD, ROWS), F32),
                pltpu.VMEM((ROWS, HD), BF16),
                pltpu.VMEM((CHEADS, 2 * UNIT, HD), BF16),
                pltpu.VMEM((UNIT, n_chip * OUT_COLS), BF16),
                pltpu.VMEM((2, UNIT, n_chip * OUT_COLS), BF16),
                pltpu.VMEM((n_chip, OUT_COLS, CHEADS * HD), BF16),
                dma((4,)), dma((4,)), dma((4,)),
                dma((REACH, SLOTS)), dma((REACH, CHUNKS)),
                dma((REACH, SLOTS)), dma((REACH, CHUNKS)),
                dma((REACH, SLOTS)), dma((REACH, CHUNKS)),
                dma((OWN, 2)), dma((OWN,)),
                dma((OWN, 2)), dma((OWN, 2)),
                dma((1,)), dma((1,)),
                dma((len(POOLED), n_chip)), dma((len(POOLED), n_sub)),
                dma((18,)), dma((2,)),
                dma((n_ctx,)), dma((n_ctx,)),
                dma((n_sub,)), dma((CHEADS,)),
                dma((1,)), dma((1,)),
                dma((n_chip,)), dma((n_chip,)),
                dma((n_chip,)), dma((n_chip,)),
            ],
            compiler_params=pltpu.CompilerParams(
                collective_id=0, has_side_effects=True, vmem_limit_bytes=60 * 2**20
            ),
        )(q, k, v, stream, pf, pc, uf, uc, ng, wq.T, wo.T)

    rows = P(("ctx", "sub"), None)
    return jax.shard_map(
        shards,
        mesh=mesh,
        in_specs=(rows, rows, rows, rows, P(), P(), P(), P(), P(), P(None, "sub"), P(None, "sub")),
        out_specs=rows,
        check_vma=False,
    )
```
